32 devices in a mesh: row: 8 (over y, x, core), col: 4 (over z).
Axes of the slice: x: 2, y: 2, z: 4, core: 2. Of those that a mesh axis runs over, the one named last changes fastest.
Arguments:
- site_cells: int32 [3, 1, 4096], P(None, None, 'row'), may hold values from 0 to 47
- site_scale: float32 [1, 4096], P(None, 'row'), may hold values from 0.3 to 3
- panel: int32 [1], replicated, may hold values from 0 to 7
Outputs:
- lower_panel: float32 [1, 4096, 512], P(None, 'row', 'col')
- trailing: bfloat16 [1, 4096, 2, 2048], P(None, 'row', None, 'col')
The draws below stay inside these ranges and needn't reach their ends.
All inputs are finite; a program needn't handle non-finite values.
Results may differ from the reference program's by a relative error of at most 0.002.
Values sent between devices are 32-bit elements; how exact they have to be, the bound alone decides.
No kernel may reach another device: no remote copies, remote signals or barrier semaphores. Data moves between devices by JAX's collectives and lax.ppermute only.
A program may use at most 64 MiB of HBM per device.

```python
import math
import jax
import jax.numpy as jnp
from jax import lax

NB = 512
TR = 1
TC = 2
N_ROW = 8
N_COL = 4


def place_ends(drawn, stream_key, smallest, top_value):
    index_at = [jax.random.randint(jax.random.fold_in(stream_key, axis), (), 0, length) for axis, length in enumerate(drawn.shape)]
    widest = drawn.shape.index(max(drawn.shape))
    next_to = index_at[:widest] + [(index_at[widest] + 1) % drawn.shape[widest]] + index_at[widest + 1:]
    return drawn.at[tuple(index_at)].set(smallest).at[tuple(next_to)].set(top_value)


def steps_of(stream_key, shape, split, smallest, top_value):
    level = 1.0
    for axis_at, shards_of in split:
        draws = jax.random.uniform(jax.random.fold_in(jax.random.fold_in(stream_key, 6), axis_at), (shards_of,), jnp.float32, smallest / len(split), top_value / len(split))
        level = level * jnp.repeat(jnp.exp(draws), shape[axis_at] // shards_of).reshape((-1,) + (1,) * (len(shape) - 1 - axis_at))
    return level


def setup_inputs(seed: int = 0) -> dict:
    splits = jax.random.split(jax.random.key(seed), 4)
    return {
        "site_cells": place_ends(jax.random.randint(splits[0], (3, TR, N_ROW * NB), 0, 48), jax.random.fold_in(splits[0], 1), 0, 47).astype(jnp.int32),
        "site_scale": jnp.clip(jnp.exp(math.log(3.0) - 2.3025851 * jax.random.uniform(splits[1], (TR, N_ROW * NB), jnp.float32) ** steps_of(splits[1], (TR, N_ROW * NB), ((1, 8),), -0.2, 0.2)), 0.3, 3.0),
        "panel": jax.random.randint(splits[2], (1,), 0, TR * N_ROW).astype(jnp.int32),
    }


stretch = (1.0, 1.0, 2.0)
nugget = 0.25
inv_length = 1.7320508075688772 / 12.0

def covariance(row_cells, row_scale, row_index, col_cells, col_scale, col_index):
    squared = jnp.zeros((row_cells.shape[1], col_cells.shape[1]), jnp.float32)
    for axis_id in range(3):
        delta = (row_cells[axis_id][:, None] - col_cells[axis_id][None, :]) * stretch[axis_id]
        squared = squared + delta * delta
    radius = inv_length * jnp.sqrt(squared)
    kernel = (1.0 + radius) * jnp.exp(-radius)
    kernel = kernel + nugget * (row_index[:, None] == col_index[None, :]).astype(jnp.float32)
    return row_scale[:, None] * col_scale[None, :] * kernel

def reference(site_cells, site_scale, panel):
    tiles = TR * N_ROW
    cells = site_cells.astype(jnp.float32).reshape(3, tiles * NB)
    scales = site_scale.reshape(tiles * NB)
    index = jnp.arange(tiles * NB, dtype=jnp.int32)
    pivot = panel[0]
    start = (pivot * NB).astype(jnp.int32)
    piv_cells = lax.dynamic_slice_in_dim(cells, start, NB, 1)
    piv_scale = lax.dynamic_slice_in_dim(scales, start, NB, 0)
    piv_index = lax.dynamic_slice_in_dim(index, start, NB, 0)
    block = covariance(piv_cells, piv_scale, piv_index, piv_cells, piv_scale, piv_index)
    factor = jnp.linalg.cholesky(block)
    inverse = jax.scipy.linalg.solve_triangular(factor, jnp.eye(NB, dtype=jnp.float32), lower=True)

    def panel_tile(tile):
        first = (tile * NB).astype(jnp.int32)
        rows = covariance(lax.dynamic_slice_in_dim(cells, first, NB, 1), lax.dynamic_slice_in_dim(scales, first, NB, 0), lax.dynamic_slice_in_dim(index, first, NB, 0), piv_cells, piv_scale, piv_index)
        return jnp.dot(rows, inverse.T, precision=lax.Precision.HIGHEST)
    lower = lax.map(panel_tile, jnp.arange(tiles, dtype=jnp.int32))
    lower_flat = lower.reshape(tiles * NB, NB)

    def trailing_tile(tile):
        first = (tile * NB).astype(jnp.int32)
        rows = covariance(lax.dynamic_slice_in_dim(cells, first, NB, 1), lax.dynamic_slice_in_dim(scales, first, NB, 0), lax.dynamic_slice_in_dim(index, first, NB, 0), cells, scales, index)
        mine = lax.dynamic_index_in_dim(lower, tile, 0, keepdims=False)
        return (rows - jnp.dot(mine, lower_flat.T, precision=lax.Precision.HIGHEST)).astype(jnp.bfloat16)
    update = lax.map(trailing_tile, jnp.arange(tiles, dtype=jnp.int32))
    return (lower.reshape(TR, N_ROW * NB, NB), update.reshape(TR, N_ROW * NB, TC, N_COL * NB))
```

```python
import functools

import jax
import jax.numpy as jnp
from jax import lax
from jax.experimental import pallas as pl
from jax.experimental.pallas import tpu as pltpu
from jax.sharding import PartitionSpec as P

nugget = 0.25
inv_length = 1.7320508075688772 / 12.0
BLOCK = 128
PANEL = 16
HIGH = lax.Precision.HIGH


def iota(shape, axis):
    return lax.broadcasted_iota(jnp.int32, shape, axis)


def over_rows(tile, row):
    return jnp.broadcast_to(tile[row : row + 1, :], tile.shape)


def over_lanes(tile, lane):
    return jnp.broadcast_to(tile[:, lane : lane + 1], tile.shape)


def inverse_factor(tiles):
    tiles = list(tiles)
    count = len(tiles)
    groups = PANEL // 8
    lane = iota((8, BLOCK), 1)
    sub = iota((8, BLOCK), 0)
    result = [None] * count
    for panel in range(BLOCK // PANEL):
        first = panel * groups
        start = panel * PANEL
        inside = (lane >= start) & (lane < start + PANEL)
        columns = [[over_lanes(tiles[first + u], start + j) for u in range(groups)] for j in range(PANEL)]
        rows = [
            jnp.where(inside, (lane == start + 8 * u + sub).astype(jnp.float32), tiles[first + u])
            for u in range(groups)
        ]
        done = [jnp.zeros((8, BLOCK), jnp.float32)] * groups
        for j in range(PANEL):
            t, s = divmod(j, 8)
            pivot = over_rows(columns[j][t], s)
            reciprocal = 1.0 / pivot
            done[t] = jnp.where(sub == s, rows[t] * lax.rsqrt(pivot), done[t])
            factor = [columns[j][u] * reciprocal for u in range(groups)]
            factor[t] = jnp.where(sub == s, 1.0 - reciprocal, factor[t])
            for k in range(j + 1, PANEL):
                row = over_rows(columns[k][t], s)
                for u in range(groups):
                    columns[k][u] = columns[k][u] - factor[u] * row
            row = over_rows(rows[t], s)
            for u in range(groups):
                rows[u] = rows[u] - factor[u] * row
        for u in range(groups):
            result[first + u] = jnp.where(lane <= start + 8 * u + sub, done[u], 0.0)
        for g in range(first + groups, count):
            total = jnp.where(inside, 0.0, tiles[g])
            for j in range(PANEL):
                total = total - over_lanes(tiles[g], start + j) * over_rows(rows[j // 8], j % 8)
            tiles[g] = total
    return result


def features(sites, left):
    x, y, z = sites[0:1, :], sites[1:2, :], 2.0 * sites[2:3, :]
    norm = x * x + y * y + z * z
    coarse = jnp.floor(norm * (1.0 / 64.0)) * 64.0
    fine = norm - coarse
    one = jnp.ones_like(x)
    if left:
        parts = (-2.0 * x, -2.0 * y, -2.0 * z, one, one, coarse, fine, 0.0 * one)
    else:
        parts = (x, y, z, coarse, fine, one, one, 0.0 * one)
    return jnp.concatenate(parts, axis=0)


def across(left, right, precision=None):
    return lax.dot_general(
        left, right, (((0,), (0,)), ((), ())), precision=precision, preferred_element_type=jnp.float32
    )


def matern(squared):
    radius = inv_length * jnp.sqrt(squared)
    return (1.0 + radius) * jnp.exp(-radius)


def kernel(n_col, share, place, sites, lower, update, work, inverse):
    width = sites.shape[2]
    tiles = update.shape[1] // width
    pivot, my_row, my_col = place[0], place[1], place[2]
    piv = sites[pivot]
    piv_left = features(piv[:3], True)
    ids = [pivot, my_row] + [m * n_col + my_col for m in range(tiles)]
    blocks = [sites[i] for i in ids]
    rights = [features(b[:3], False) for b in blocks]
    eye = iota((BLOCK, width), 0)
    for slot, right in enumerate(rights):
        for chunk in range(width // BLOCK):
            rows = slice(chunk * BLOCK, (chunk + 1) * BLOCK)
            value = matern(across(piv_left[:, rows], right))
            on_diagonal = (eye + chunk * BLOCK == iota((BLOCK, width), 1)) & (ids[slot] == pivot)
            work[rows, slot * width : (slot + 1) * width] = value + jnp.where(on_diagonal, nugget, 0.0)
    total = work.shape[1]
    for k in range(width // BLOCK):
        here = slice(k * BLOCK, (k + 1) * BLOCK)
        found = inverse_factor([work[k * BLOCK + 8 * g : k * BLOCK + 8 * g + 8, here] for g in range(BLOCK // 8)])
        for g in range(BLOCK // 8):
            inverse[8 * g : 8 * g + 8, :] = found[g]
        after = (k + 1) * BLOCK
        for start in range(after, total, 512):
            part = slice(start, min(start + 512, total))
            work[here, part] = jnp.dot(
                inverse[...], work[here, part], precision=HIGH, preferred_element_type=jnp.float32
            )
        for row in range(after, width, BLOCK):
            rows = slice(row, row + BLOCK)
            for start in range(after, total, 512):
                part = slice(start, min(start + 512, total))
                work[rows, part] = work[rows, part] - across(work[here, rows], work[here, part], HIGH)
    mine = blocks[1]
    my_left = features(mine[:3], True)
    my_scale = jnp.broadcast_to(mine[3:4, :], (8, width)).T[:, 0:1]
    for chunk in range(width // BLOCK):
        rows = slice(chunk * BLOCK, (chunk + 1) * BLOCK)
        own = slice(width + chunk * BLOCK, width + (chunk + 1) * BLOCK)
        for m in range(tiles):
            cols = slice((2 + m) * width, (3 + m) * width)
            value = matern(across(my_left[:, rows], rights[2 + m]))
            on_diagonal = (eye + chunk * BLOCK == iota((BLOCK, width), 1)) & (ids[2 + m] == my_row)
            value = value + jnp.where(on_diagonal, nugget, 0.0)
            value = value - across(work[:, own], work[:, cols], HIGH)
            value = value * my_scale[rows, :] * blocks[2 + m][3:4, :]
            update[rows, m * width : (m + 1) * width] = value.astype(jnp.bfloat16)
        if share % BLOCK == 0:
            at = pl.multiple_of(my_col * share, BLOCK)
            lower[rows, :] = work[pl.ds(at, share), own].T * my_scale[rows, :]
        else:
            lower[rows, :] = work[:, own].T * my_scale[rows, :]


def on_device(site_cells, site_scale, panel):
    width = site_cells.shape[2]
    n_row = lax.axis_size("row")
    n_col = lax.axis_size("col")
    my_row = lax.axis_index("row")
    my_col = lax.axis_index("col")
    tiles = n_row // n_col
    share = width // n_col
    packed = jnp.concatenate([site_cells.astype(jnp.float32).reshape(3, width), site_scale], axis=0)
    sites = lax.all_gather(packed, "row", axis=0)
    place = jnp.stack([panel[0], my_row, my_col]).astype(jnp.int32)
    held = share if share % BLOCK == 0 else width
    vmem = pl.BlockSpec(memory_space=pltpu.VMEM)
    lower, update = pl.pallas_call(
        functools.partial(kernel, n_col, share),
        out_shape=(
            jax.ShapeDtypeStruct((width, held), jnp.float32),
            jax.ShapeDtypeStruct((width, tiles * width), jnp.bfloat16),
        ),
        in_specs=[pl.BlockSpec(memory_space=pltpu.SMEM), vmem],
        out_specs=(vmem, vmem),
        scratch_shapes=[
            pltpu.VMEM((width, (2 + tiles) * width), jnp.float32),
            pltpu.VMEM((BLOCK, BLOCK), jnp.float32),
        ],
        compiler_params=pltpu.CompilerParams(vmem_limit_bytes=40 * 2**20),
    )(place, sites)
    if held != share:
        lower = lax.dynamic_slice_in_dim(lower, my_col * share, share, 1)
    return lower[None], update.reshape(1, width, tiles, width)


def solution(mesh):
    placed = (P(None, None, "row"), P(None, "row"), P())
    return jax.shard_map(
        on_device,
        mesh=mesh,
        in_specs=placed,
        out_specs=(P(None, "row", "col"), P(None, "row", None, "col")),
        check_vma=False,
    )
```

```python
import functools

import jax
import jax.numpy as jnp
from jax import lax
from jax.experimental import pallas as pl
from jax.experimental.pallas import tpu as pltpu
from jax.sharding import PartitionSpec as P

nugget = 0.25
inv_length = 1.7320508075688772 / 12.0
log2_e = 1.4426950408889634
BLOCK = 128
PANEL = 16
HIGH = lax.Precision.HIGH


def iota(shape, axis):
    return lax.broadcasted_iota(jnp.int32, shape, axis)


def over_rows(tile, row):
    return jnp.broadcast_to(tile[row : row + 1, :], tile.shape)


def over_lanes(tile, lane):
    return jnp.broadcast_to(tile[:, lane : lane + 1], tile.shape)


def tree_sum(parts):
    while len(parts) > 1:
        parts = [a + b for a, b in zip(parts[0::2], parts[1::2])]
    return parts[0]


def eliminate(tiles, inverse):
    tiles = list(tiles)
    count = len(tiles)
    groups = PANEL // 8
    lane = iota((8, BLOCK), 1)
    sub = iota((8, BLOCK), 0)
    nothing = jnp.zeros((8, BLOCK), jnp.float32)
    for panel in range(BLOCK // PANEL):
        first = panel * groups
        start = panel * PANEL
        inside = (lane >= start) & (lane < start + PANEL)
        columns = [[over_lanes(tiles[first + u], start + j) for u in range(groups)] for j in range(PANEL)]
        rows = [
            jnp.where(inside, (lane == start + 8 * u + sub).astype(jnp.float32), tiles[first + u])
            for u in range(groups)
        ]
        near = range(first + groups, min(count, first + 2 * groups))
        below = {g: [over_lanes(tiles[g], start + j) for j in range(PANEL)] for g in near}
        done = [nothing] * groups
        for j in range(0, PANEL, 2):
            t, s = divmod(j, 8)
            left, right = columns[j], columns[j + 1]
            a, b, d = over_rows(left[t], s), over_rows(right[t], s), over_rows(right[t], s + 1)
            scale = 1.0 / (a * d - b * b)
            one = [(left[u] * d - right[u] * b) * scale for u in range(groups)]
            two = [(right[u] * a - left[u] * b) * scale for u in range(groups)]
            a_new, b_new, d_new = a * scale, b * scale, d * scale
            one[t] = jnp.where(sub == s, 1.0 - d_new, jnp.where(sub == s + 1, b_new, one[t]))
            two[t] = jnp.where(sub == s, b_new, jnp.where(sub == s + 1, 1.0 - a_new, two[t]))
            top, low = over_rows(rows[t], s), over_rows(rows[t], s + 1)
            ratio = b / a
            low_done = (low - ratio * top) * lax.rsqrt(d - ratio * b)
            done[t] = jnp.where(sub == s, top * lax.rsqrt(a), jnp.where(sub == s + 1, low_done, done[t]))
            for k in range(j + 2, PANEL):
                x, y = over_rows(columns[k][t], s), over_rows(columns[k][t], s + 1)
                for u in range(groups):
                    columns[k][u] = columns[k][u] - (one[u] * x + two[u] * y)
            for u in range(groups):
                rows[u] = rows[u] - (one[u] * top + two[u] * low)
            yield
        for u in range(groups):
            at = start + 8 * u
            inverse[at : at + 8, :] = jnp.where(lane <= at + sub, done[u], 0.0)
        for g in near:
            change = tree_sum([below[g][j] * over_rows(rows[j // 8], j % 8) for j in range(PANEL)])
            tiles[g] = jnp.where(inside, 0.0, tiles[g]) - change
        if near and near[-1] + 1 < count:
            far = near[-1] + 1
            padded = jnp.concatenate([nothing] * first + rows + [nothing] * (count - first - groups), axis=0)
            change = times(jnp.concatenate(tiles[far:], axis=0), padded)
            for i, g in enumerate(range(far, count)):
                tiles[g] = jnp.where(inside, 0.0, tiles[g]) - change[8 * i : 8 * i + 8, :]


def features(sites, left):
    x, y, z = sites[0:1, :], sites[1:2, :], 2.0 * sites[2:3, :]
    norm = x * x + y * y + z * z
    coarse = jnp.floor(norm * (1.0 / 64.0)) * 64.0
    fine = norm - coarse
    one = jnp.ones_like(x)
    if left:
        parts = (-2.0 * x, -2.0 * y, -2.0 * z, one, one, coarse, fine, 0.0 * one)
    else:
        parts = (x, y, z, coarse, fine, one, one, 0.0 * one)
    return jnp.concatenate(parts, axis=0)


def times(left, right, precision=HIGH):
    return jnp.dot(left, right, precision=precision, preferred_element_type=jnp.float32)


def matern(left, right):
    squared = times(left, right, None)
    root = squared * lax.rsqrt(jnp.maximum(squared, 1e-30))
    return (1.0 + inv_length * root) * jnp.exp2((-inv_length * log2_e) * root)


def split(value):
    high = value.astype(jnp.bfloat16)
    return high, (value - high.astype(jnp.float32)).astype(jnp.bfloat16)


def kernel(n_col, share, place, sites, lower, update, block, work, rest, left3, right3, inverses, corner, scales, found):
    width = sites.shape[2]
    tiles = update.shape[1] // width
    count = width // BLOCK
    half = width // 2
    pivot, my_row, my_col = place[0], place[1], place[2]
    ids = [my_row] + [m * n_col + my_col for m in range(tiles)]
    piv = sites[pivot]
    blocks = [sites[i] for i in ids]
    found[0] = features(piv, True).T
    found[1] = features(blocks[0], True).T
    rights = [features(b, False) for b in [piv] + blocks]
    for i, right in enumerate(rights):
        corner[i] = right

    def at(k):
        return slice(k * BLOCK, (k + 1) * BLOCK)

    def nuggets(row, col, shape, amount):
        same = iota(shape, 0) + row == iota(shape, 1) + col
        return jnp.where(same, amount, 0.0)

    def pivot_tile(i, j):
        value = matern(found[0, at(i), :], corner[0, :, at(j)])
        block[at(i), at(j)] = value + nuggets(0, 0, value.shape, nugget) if i == j else value

    wide = 2 * BLOCK
    pieces = width // wide

    def covariance(side, i, slot, piece, is_same):
        cols = slice(piece * wide, (piece + 1) * wide)
        value = matern(found[side, at(i), :], corner[1 + slot, :, cols])
        if piece * wide <= i * BLOCK < (piece + 1) * wide:
            value = value + nuggets(i * BLOCK, piece * wide, value.shape, jnp.where(is_same, nugget, 0.0))
        return value

    def panel_tile(i, slot, piece):
        cols = slice(slot * width + piece * wide, slot * width + (piece + 1) * wide)
        work[at(i), cols] = covariance(0, i, slot, piece, ids[slot] == pivot)

    def rest_tile(i, m, piece):
        cols = slice(m * width + piece * wide, m * width + (piece + 1) * wide)
        rest[at(i), cols] = covariance(1, i, 1 + m, piece, ids[1 + m] == my_row)

    def row_scale():
        scales[...] = jnp.broadcast_to(jnp.broadcast_to(blocks[0][3:4, :], (8, width)).T[:, 0:1], scales.shape)

    def solve(rows, cols, inverse):
        work[rows, cols] = times(inverse[...], work[rows, cols])

    def subtract(rows, cols, by, factor):
        work[rows, cols] = work[rows, cols] - times(factor(), work[by, cols])

    def keep_left(h, k):
        high, low = split(work[at(k), 0:width].T)
        j = k % 2 * BLOCK
        for place_at, part in ((0, high), (half, high), (2 * half, low)):
            left3[h, :, place_at + j : place_at + j + BLOCK] = part

    def keep_right(h, k, cols):
        high, low = split(work[at(k), slice(width + cols.start, width + cols.stop)])
        j = k % 2 * BLOCK
        for place_at, part in ((0, high), (half, low), (2 * half, high)):
            right3[h, place_at + j : place_at + j + BLOCK, cols] = part

    def reduce(h, rows, cols):
        return rest[rows, cols] - times(left3[h, rows, :], right3[h, :, cols], None)

    def first_half(rows, cols):
        rest[rows, cols] = reduce(0, rows, cols)

    def todo(task, *given):
        return functools.partial(task, *given)

    everything = work.shape[1]
    strips = [slice(c, c + wide) for c in range(0, everything, wide)]
    out_strips = [slice(c, c + wide) for c in range(0, tiles * width, wide)]
    halves = [slice(0, half), slice(half, width)]
    couple = slice(0, 2 * BLOCK)
    later = slice(2 * BLOCK, 4 * BLOCK)

    def big_factor():
        return block[couple, later].T

    shadows = [[] for _ in range(count)]
    shadows[0] += [todo(pivot_tile, i, j) for i in range(count) for j in range(i, count) if i + j]
    shadows[0] += [todo(panel_tile, i, s, p) for i in range(2) for s in range(1 + tiles) for p in range(pieces)]
    shadows[0] += [row_scale]
    shadows[1] += [todo(panel_tile, i, s, p) for i in range(2, count) for s in range(1 + tiles) for p in range(pieces)]
    rest_tiles = [todo(rest_tile, i, m, p) for i in range(count) for m in range(tiles) for p in range(pieces)]
    shadows[1] += rest_tiles[: len(rest_tiles) // 2]
    shadows[2] += [todo(solve, couple, c, inverses.at[4]) for c in strips]
    shadows[2] += [todo(subtract, later, c, couple, big_factor) for c in strips]
    shadows[2] += rest_tiles[len(rest_tiles) // 2 :]
    shadows[2] += [todo(keep_left, 0, k) for k in range(2)]
    shadows[2] += [todo(keep_right, 0, k, c) for c in out_strips for k in range(2)]
    shadows[3] += [todo(solve, at(2), c, inverses.at[2, 0:BLOCK, 0:BLOCK]) for c in strips]
    shadows[3] += [todo(subtract, at(3), c, at(2), lambda: block[at(2), at(3)].T) for c in strips]
    shadows[3] += [todo(keep_left, 1, 2)]
    shadows[3] += [todo(keep_right, 1, 2, c) for c in out_strips]
    shadows[3] += [todo(first_half, r, c) for c in out_strips for r in halves]

    pivot_tile(0, 0)
    steps = BLOCK // 2
    for k in range(count):
        inverse = inverses.at[k, 0:BLOCK, 0:BLOCK]
        tasks = shadows[k]
        given = 0
        for step, _ in enumerate(
            eliminate([block[k * BLOCK + 8 * g : k * BLOCK + 8 * g + 8, at(k)] for g in range(BLOCK // 8)], inverse)
        ):
            goal = len(tasks) * (step + 1) // steps
            for task in tasks[given:goal]:
                task()
            given = goal
        after = slice((k + 1) * BLOCK, width)
        if k + 1 < count:
            solved = times(inverse[...], block[at(k), after])
            block[at(k), after] = solved
            for i in range(k + 1, count):
                cols = slice(i * BLOCK, width)
                here = slice((i - k - 1) * BLOCK, (i - k) * BLOCK)
                block[at(i), cols] = block[at(i), cols] - times(solved[:, here].T, solved[:, (i - k - 1) * BLOCK :])
        if k == 1:
            across = times(inverse[...], times(block[at(0), at(1)].T, inverses[0, 0:BLOCK, 0:BLOCK]))
            inverses[4, 0:BLOCK, 0:BLOCK] = inverses[0, 0:BLOCK, 0:BLOCK]
            inverses[4, 0:BLOCK, BLOCK : 2 * BLOCK] = jnp.zeros((BLOCK, BLOCK), jnp.float32)
            inverses[4, BLOCK : 2 * BLOCK, 0:BLOCK] = -across
            inverses[4, BLOCK : 2 * BLOCK, BLOCK : 2 * BLOCK] = inverse[...]
    for c in strips:
        solve(at(3), c, inverses.at[3, 0:BLOCK, 0:BLOCK])
    keep_left(1, 3)
    for c in out_strips:
        keep_right(1, 3, c)
        col_scale = blocks[1 + c.start // width][3:4, c.start % width : c.start % width + wide]
        for r in halves:
            value = reduce(1, r, c)
            by_row = jnp.concatenate([scales[r, :]] * (wide // BLOCK), axis=1)
            update[r, c] = (value * by_row * col_scale).astype(jnp.bfloat16)
    if share % BLOCK == 0:
        start = pl.multiple_of(my_col * share, BLOCK)
        lower[...] = work[pl.ds(start, share), 0:width].T * jnp.concatenate([scales[...]] * (share // BLOCK), axis=1)
    else:
        lower[...] = work[:, 0:width].T * jnp.concatenate([scales[...]] * count, axis=1)


def on_device(site_cells, site_scale, panel):
    width = site_cells.shape[2]
    n_row = lax.axis_size("row")
    n_col = lax.axis_size("col")
    my_row = lax.axis_index("row")
    my_col = lax.axis_index("col")
    tiles = n_row // n_col
    share = width // n_col
    packed = jnp.concatenate([site_cells.astype(jnp.float32).reshape(3, width), site_scale], axis=0)
    sites = lax.all_gather(packed, "row", axis=0)
    place = jnp.stack([panel[0], my_row, my_col]).astype(jnp.int32)
    held = share if share % BLOCK == 0 else width
    vmem = pl.BlockSpec(memory_space=pltpu.VMEM)
    lower, update = pl.pallas_call(
        functools.partial(kernel, n_col, share),
        out_shape=(
            jax.ShapeDtypeStruct((width, held), jnp.float32),
            jax.ShapeDtypeStruct((width, tiles * width), jnp.bfloat16),
        ),
        in_specs=[pl.BlockSpec(memory_space=pltpu.SMEM), vmem],
        out_specs=(vmem, vmem),
        scratch_shapes=[
            pltpu.VMEM((width, width), jnp.float32),
            pltpu.VMEM((width, (1 + tiles) * width), jnp.float32),
            pltpu.VMEM((width, tiles * width), jnp.float32),
            pltpu.VMEM((2, width, 3 * width // 2), jnp.bfloat16),
            pltpu.VMEM((2, 3 * width // 2, tiles * width), jnp.bfloat16),
            pltpu.VMEM((5, 2 * BLOCK, 2 * BLOCK), jnp.float32),
            pltpu.VMEM((2 + tiles, 8, width), jnp.float32),
            pltpu.VMEM((width, BLOCK), jnp.float32),
            pltpu.VMEM((2, width, 8), jnp.float32),
        ],
        compiler_params=pltpu.CompilerParams(vmem_limit_bytes=40 * 2**20),
    )(place, sites)
    if held != share:
        lower = lax.dynamic_slice_in_dim(lower, my_col * share, share, 1)
    return lower[None], update.reshape(1, width, tiles, width)


def solution(mesh):
    placed = (P(None, None, "row"), P(None, "row"), P())
    return jax.shard_map(
        on_device,
        mesh=mesh,
        in_specs=placed,
        out_specs=(P(None, "row", "col"), P(None, "row", None, "col")),
        check_vma=False,
    )
```

```python
import functools

import jax
import jax.numpy as jnp
from jax import lax
from jax.experimental import pallas as pl
from jax.experimental.pallas import tpu as pltpu
from jax.sharding import PartitionSpec as P

nugget = 0.25
inv_length = 1.7320508075688772 / 12.0
log2_e = 1.4426950408889634
BLOCK = 128
PANEL = 16
HIGH = lax.Precision.HIGH


def iota(shape, axis):
    return lax.broadcasted_iota(jnp.int32, shape, axis)


def over_rows(tile, row):
    return jnp.broadcast_to(tile[row : row + 1, :], tile.shape)


def over_lanes(tile, lane):
    return jnp.broadcast_to(tile[:, lane : lane + 1], tile.shape)


def tree_sum(parts):
    while len(parts) > 1:
        parts = [a + b for a, b in zip(parts[0::2], parts[1::2])]
    return parts[0]


def eliminate(tiles, inverse):
    tiles = list(tiles)
    count = len(tiles)
    groups = PANEL // 8
    lane = iota((8, BLOCK), 1)
    sub = iota((8, BLOCK), 0)
    nothing = jnp.zeros((8, BLOCK), jnp.float32)
    for panel in range(BLOCK // PANEL):
        first = panel * groups
        start = panel * PANEL
        inside = (lane >= start) & (lane < start + PANEL)
        columns = [[over_lanes(tiles[first + u], start + j) for u in range(groups)] for j in range(PANEL)]
        rows = [
            jnp.where(inside, (lane == start + 8 * u + sub).astype(jnp.float32), tiles[first + u])
            for u in range(groups)
        ]
        near = range(first + groups, min(count, first + 2 * groups))
        below = {g: [over_lanes(tiles[g], start + j) for j in range(PANEL)] for g in near}
        done = [nothing] * groups
        for j in range(0, PANEL, 2):
            t, s = divmod(j, 8)
            left, right = columns[j], columns[j + 1]
            a, b, d = over_rows(left[t], s), over_rows(right[t], s), over_rows(right[t], s + 1)
            area = a * d - b * b
            scale = 1.0 / area
            one = [left[u] * d - right[u] * b for u in range(groups)]
            two = [right[u] * a - left[u] * b for u in range(groups)]
            one[t] = jnp.where(sub == s, area - d, jnp.where(sub == s + 1, b, one[t]))
            two[t] = jnp.where(sub == s, b, jnp.where(sub == s + 1, area - a, two[t]))
            top, low = over_rows(rows[t], s), over_rows(rows[t], s + 1)
            low_done = (a * low - b * top) * lax.rsqrt(a * area)
            done[t] = jnp.where(sub == s, top * lax.rsqrt(a), jnp.where(sub == s + 1, low_done, done[t]))
            one_scaled = [value * scale for value in one]
            two_scaled = [value * scale for value in two]
            for k in range(j + 2, PANEL):
                x, y = over_rows(left[k // 8], k % 8), over_rows(right[k // 8], k % 8)
                for u in range(groups):
                    if k < j + 4:
                        change = (one[u] * x + two[u] * y) * scale
                    else:
                        change = one_scaled[u] * x + two_scaled[u] * y
                    columns[k][u] = columns[k][u] - change
            for u in range(groups):
                rows[u] = rows[u] - (one[u] * top + two[u] * low) * scale
            yield
        for u in range(groups):
            at = start + 8 * u
            inverse[at : at + 8, :] = jnp.where(lane <= at + sub, done[u], 0.0)
        for g in near:
            change = tree_sum([below[g][j] * over_rows(rows[j // 8], j % 8) for j in range(PANEL)])
            tiles[g] = jnp.where(inside, 0.0, tiles[g]) - change
        if near and near[-1] + 1 < count:
            far = near[-1] + 1
            padded = jnp.concatenate([nothing] * first + rows + [nothing] * (count - first - groups), axis=0)
            change = times(jnp.concatenate(tiles[far:], axis=0), padded)
            for i, g in enumerate(range(far, count)):
                tiles[g] = jnp.where(inside, 0.0, tiles[g]) - change[8 * i : 8 * i + 8, :]


def features(sites, left):
    x, y, z = sites[0:1, :], sites[1:2, :], 2.0 * sites[2:3, :]
    norm = x * x + y * y + z * z
    coarse = jnp.floor(norm * (1.0 / 64.0)) * 64.0
    fine = norm - coarse
    one = jnp.ones_like(x)
    if left:
        parts = (-2.0 * x, -2.0 * y, -2.0 * z, one, one, coarse, fine, 0.0 * one)
    else:
        parts = (x, y, z, coarse, fine, one, one, 0.0 * one)
    return jnp.concatenate(parts, axis=0)


def times(left, right, precision=HIGH):
    return jnp.dot(left, right, precision=precision, preferred_element_type=jnp.float32)


def matern(left, right):
    squared = times(left, right, None)
    root = squared * lax.rsqrt(jnp.maximum(squared, 1e-30))
    return (1.0 + inv_length * root) * jnp.exp2((-inv_length * log2_e) * root)


def split(value):
    high = value.astype(jnp.bfloat16)
    return high, (value - high.astype(jnp.float32)).astype(jnp.bfloat16)


def pack(cells, scale, packed):
    for axis in range(3):
        packed[axis : axis + 1, :] = cells[axis].astype(jnp.float32)
    packed[3:4, :] = scale[...]


def kernel(n_col, share, n_sites, place, *refs):
    arrived = refs[:n_sites]
    lower, update, block, work, rest, left3, right3, inverses, corner, scales, found, sites = refs[n_sites:]
    width = sites.shape[2]
    tiles = update.shape[1]
    count = width // BLOCK
    half = width // 2
    pivot, my_row, my_col = place[0], place[1], place[2]
    ids = [my_row] + [m * n_col + my_col for m in range(tiles)]
    if n_sites == 1:
        sites[...] = arrived[0][...]
        found_at = lambda i: i
    else:
        for i in range(n_sites):
            sites[i] = arrived[i][...]
        found_at = lambda i: i ^ my_row
    piv = sites[found_at(pivot)]
    blocks = [sites[found_at(i)] for i in ids]
    found[0] = features(piv, True).T
    found[1] = features(blocks[0], True).T
    rights = [features(b, False) for b in [piv] + blocks]
    for i, right in enumerate(rights):
        corner[i] = right

    def at(k):
        return slice(k * BLOCK, (k + 1) * BLOCK)

    def nuggets(row, col, shape, amount):
        same = iota(shape, 0) + row == iota(shape, 1) + col
        return jnp.where(same, amount, 0.0)

    def pivot_tile(i, j):
        value = matern(found[0, at(i), :], corner[0, :, at(j)])
        block[at(i), at(j)] = value + nuggets(0, 0, value.shape, nugget) if i == j else value

    wide = 2 * BLOCK
    pieces = width // wide

    def covariance(side, i, slot, piece, is_same):
        cols = slice(piece * wide, (piece + 1) * wide)
        value = matern(found[side, at(i), :], corner[1 + slot, :, cols])
        if piece * wide <= i * BLOCK < (piece + 1) * wide:
            value = value + nuggets(i * BLOCK, piece * wide, value.shape, jnp.where(is_same, nugget, 0.0))
        return value

    def panel_tile(i, slot, piece):
        cols = slice(slot * width + piece * wide, slot * width + (piece + 1) * wide)
        work[at(i), cols] = covariance(0, i, slot, piece, ids[slot] == pivot)

    def rest_tile(i, m, piece):
        cols = slice(m * width + piece * wide, m * width + (piece + 1) * wide)
        rest[at(i), cols] = covariance(1, i, 1 + m, piece, ids[1 + m] == my_row)

    def row_scale():
        scales[...] = jnp.broadcast_to(jnp.broadcast_to(blocks[0][3:4, :], (8, width)).T[:, 0:1], scales.shape)

    def solve(rows, cols, inverse):
        work[rows, cols] = times(inverse[...], work[rows, cols])

    def subtract(rows, cols, by, factor):
        work[rows, cols] = work[rows, cols] - times(factor(), work[by, cols])

    def keep_left(h, k):
        high, low = split(work[at(k), 0:width].T)
        j = k % 2 * BLOCK
        for place_at, part in ((0, high), (half, high), (2 * half, low)):
            left3[h, :, place_at + j : place_at + j + BLOCK] = part

    def keep_right(h, k, cols):
        high, low = split(work[at(k), slice(width + cols.start, width + cols.stop)])
        j = k % 2 * BLOCK
        for place_at, part in ((0, high), (half, low), (2 * half, high)):
            right3[h, place_at + j : place_at + j + BLOCK, cols] = part

    def reduce(h, rows, cols):
        return rest[rows, cols] - times(left3[h, rows, :], right3[h, :, cols], None)

    def first_half(rows, cols):
        rest[rows, cols] = reduce(0, rows, cols)

    def todo(task, *given):
        return functools.partial(task, *given)

    everything = work.shape[1]
    strips = [slice(c, c + wide) for c in range(0, everything, wide)]
    out_strips = [slice(c, c + wide) for c in range(0, tiles * width, wide)]
    halves = [slice(0, half), slice(half, width)]
    couple = slice(0, 2 * BLOCK)
    later = slice(2 * BLOCK, 4 * BLOCK)

    def big_factor():
        return block[couple, later].T

    shadows = [[] for _ in range(count)]
    shadows[0] += [todo(pivot_tile, i, j) for i in range(count) for j in range(i, count) if i + j]
    shadows[0] += [todo(panel_tile, i, s, p) for i in range(2) for s in range(1 + tiles) for p in range(pieces)]
    shadows[0] += [row_scale]
    shadows[1] += [todo(panel_tile, i, s, p) for i in range(2, count) for s in range(1 + tiles) for p in range(pieces)]
    rest_tiles = [todo(rest_tile, i, m, p) for i in range(count) for m in range(tiles) for p in range(pieces)]
    shadows[1] += rest_tiles[: len(rest_tiles) // 2]
    shadows[2] += [todo(solve, couple, c, inverses.at[4]) for c in strips]
    shadows[2] += [todo(subtract, later, c, couple, big_factor) for c in strips]
    shadows[2] += rest_tiles[len(rest_tiles) // 2 :]
    shadows[2] += [todo(keep_left, 0, k) for k in range(2)]
    shadows[2] += [todo(keep_right, 0, k, c) for c in out_strips for k in range(2)]
    shadows[3] += [todo(solve, at(2), c, inverses.at[2, 0:BLOCK, 0:BLOCK]) for c in strips]
    shadows[3] += [todo(subtract, at(3), c, at(2), lambda: block[at(2), at(3)].T) for c in strips]
    shadows[3] += [todo(keep_left, 1, 2)]
    shadows[3] += [todo(keep_right, 1, 2, c) for c in out_strips]
    shadows[3] += [todo(first_half, r, c) for c in out_strips for r in halves]

    pivot_tile(0, 0)
    steps = BLOCK // 2
    for k in range(count):
        inverse = inverses.at[k, 0:BLOCK, 0:BLOCK]
        tasks = shadows[k]
        given = 0
        for step, _ in enumerate(
            eliminate([block[k * BLOCK + 8 * g : k * BLOCK + 8 * g + 8, at(k)] for g in range(BLOCK // 8)], inverse)
        ):
            goal = len(tasks) * (step + 1) // steps
            for task in tasks[given:goal]:
                task()
            given = goal
        after = slice((k + 1) * BLOCK, width)
        if k + 1 < count:
            solved = times(inverse[...], block[at(k), after])
            block[at(k), after] = solved
            for i in range(k + 1, count):
                cols = slice(i * BLOCK, width)
                here = slice((i - k - 1) * BLOCK, (i - k) * BLOCK)
                block[at(i), cols] = block[at(i), cols] - times(solved[:, here].T, solved[:, (i - k - 1) * BLOCK :])
        if k == 1:
            across = times(inverse[...], times(block[at(0), at(1)].T, inverses[0, 0:BLOCK, 0:BLOCK]))
            inverses[4, 0:BLOCK, 0:BLOCK] = inverses[0, 0:BLOCK, 0:BLOCK]
            inverses[4, 0:BLOCK, BLOCK : 2 * BLOCK] = jnp.zeros((BLOCK, BLOCK), jnp.float32)
            inverses[4, BLOCK : 2 * BLOCK, 0:BLOCK] = -across
            inverses[4, BLOCK : 2 * BLOCK, BLOCK : 2 * BLOCK] = inverse[...]
    for c in strips:
        solve(at(3), c, inverses.at[3, 0:BLOCK, 0:BLOCK])
    keep_left(1, 3)
    for c in out_strips:
        keep_right(1, 3, c)
    part = BLOCK // tiles
    order = iota((BLOCK, BLOCK), 0) // tiles + iota((BLOCK, BLOCK), 0) % tiles * part
    weave = (order == iota((BLOCK, BLOCK), 1)).astype(jnp.bfloat16)
    for c in out_strips[: width // wide]:
        for r in halves:
            by_row = jnp.concatenate([scales[r, :]] * (wide // BLOCK), axis=1)
            values = []
            for m in range(tiles):
                value = reduce(1, r, slice(m * width + c.start, m * width + c.stop))
                values.append((value * by_row * blocks[1 + m][3:4, c]).astype(jnp.bfloat16))
            for row in range(0, half, part):
                stacked = jnp.concatenate([value[row : row + part, :] for value in values], axis=0)
                woven = times(weave, stacked, None).astype(jnp.bfloat16)
                update[r.start + row : r.start + row + part, :, c] = woven.reshape(part, tiles, wide)
    if share % BLOCK == 0:
        start = pl.multiple_of(my_col * share, BLOCK)
        lower[...] = work[pl.ds(start, share), 0:width].T * jnp.concatenate([scales[...]] * (share // BLOCK), axis=1)
    else:
        lower[...] = work[:, 0:width].T * jnp.concatenate([scales[...]] * count, axis=1)


def swap(value, step, count):
    return lax.ppermute(value, "row", [(i, i ^ step) for i in range(count)])


def on_device(site_cells, site_scale, panel):
    width = site_cells.shape[2]
    n_row = lax.axis_size("row")
    n_col = lax.axis_size("col")
    my_row = lax.axis_index("row")
    my_col = lax.axis_index("col")
    tiles = n_row // n_col
    share = width // n_col
    vmem = pl.BlockSpec(memory_space=pltpu.VMEM)
    packed = pl.pallas_call(
        pack,
        out_shape=jax.ShapeDtypeStruct((4, width), jnp.float32),
        in_specs=[vmem, vmem],
        out_specs=vmem,
    )(site_cells, site_scale)
    if n_row == 8:
        arrived = [packed] + [swap(packed, k, n_row) for k in range(2, n_row, 2)]
        others = [swap(value, 1, n_row) for value in arrived]
        arrived = [value for both in zip(arrived, others) for value in both]
    else:
        arrived = [lax.all_gather(packed, "row", axis=0)]
    place = jnp.stack([panel[0], my_row, my_col]).astype(jnp.int32)
    held = share if share % BLOCK == 0 else width
    lower, update = pl.pallas_call(
        functools.partial(kernel, n_col, share, len(arrived)),
        out_shape=(
            jax.ShapeDtypeStruct((width, held), jnp.float32),
            jax.ShapeDtypeStruct((width, tiles, width), jnp.bfloat16),
        ),
        in_specs=[pl.BlockSpec(memory_space=pltpu.SMEM)] + [vmem] * len(arrived),
        out_specs=(vmem, vmem),
        scratch_shapes=[
            pltpu.VMEM((width, width), jnp.float32),
            pltpu.VMEM((width, (1 + tiles) * width), jnp.float32),
            pltpu.VMEM((width, tiles * width), jnp.float32),
            pltpu.VMEM((2, width, 3 * width // 2), jnp.bfloat16),
            pltpu.VMEM((2, 3 * width // 2, tiles * width), jnp.bfloat16),
            pltpu.VMEM((5, 2 * BLOCK, 2 * BLOCK), jnp.float32),
            pltpu.VMEM((2 + tiles, 8, width), jnp.float32),
            pltpu.VMEM((width, BLOCK), jnp.float32),
            pltpu.VMEM((2, width, 8), jnp.float32),
            pltpu.VMEM((n_row, 4, width), jnp.float32),
        ],
        compiler_params=pltpu.CompilerParams(vmem_limit_bytes=40 * 2**20),
    )(place, *arrived)
    if held != share:
        lower = lax.dynamic_slice_in_dim(lower, my_col * share, share, 1)
    return lower[None], update[None]


def solution(mesh):
    placed = (P(None, None, "row"), P(None, "row"), P())
    return jax.shard_map(
        on_device,
        mesh=mesh,
        in_specs=placed,
        out_specs=(P(None, "row", "col"), P(None, "row", None, "col")),
        check_vma=False,
    )
```

```python
import functools

import jax
import jax.numpy as jnp
from jax import lax
from jax.experimental import pallas as pl
from jax.experimental.pallas import tpu as pltpu
from jax.sharding import PartitionSpec as P

nugget = 0.25
inv_length = 1.7320508075688772 / 12.0
log2_e = 1.4426950408889634
BLOCK = 128
PANEL = 16
HIGH = lax.Precision.HIGH


def iota(shape, axis):
    return lax.broadcasted_iota(jnp.int32, shape, axis)


def over_rows(tile, row):
    return jnp.broadcast_to(tile[row : row + 1, :], tile.shape)


def over_lanes(tile, lane):
    return jnp.broadcast_to(tile[:, lane : lane + 1], tile.shape)


def tree_sum(parts):
    while len(parts) > 1:
        parts = [a + b for a, b in zip(parts[0::2], parts[1::2])]
    return parts[0]


def eliminate(tiles, inverse):
    tiles = list(tiles)
    count = len(tiles)
    groups = PANEL // 8
    lane = iota((8, BLOCK), 1)
    sub = iota((8, BLOCK), 0)
    even = sub % 2 == 0
    nothing = jnp.zeros((8, BLOCK), jnp.float32)
    for panel in range(BLOCK // PANEL):
        first = panel * groups
        start = panel * PANEL
        inside = (lane >= start) & (lane < start + PANEL)
        columns = [[over_lanes(tiles[first + u], start + j) for u in range(groups)] for j in range(PANEL)]
        rows = [
            jnp.where(inside, (lane == start + 8 * u + sub).astype(jnp.float32), tiles[first + u])
            for u in range(groups)
        ]
        near = range(first + groups, min(count, first + 2 * groups))
        below = {g: [over_lanes(tiles[g], start + j) for j in range(PANEL)] for g in near}
        kept = [[nothing] * groups for _ in range(3)]
        for j in range(0, PANEL, 2):
            t, s = divmod(j, 8)
            left, right = columns[j], columns[j + 1]
            a, b, d = over_rows(left[t], s), over_rows(right[t], s), over_rows(right[t], s + 1)
            area = a * d - b * b
            scale = 1.0 / area
            one = [left[u] * d - right[u] * b for u in range(groups)]
            two = [right[u] * a - left[u] * b for u in range(groups)]
            one[t] = jnp.where(sub == s, area - d, jnp.where(sub == s + 1, b, one[t]))
            two[t] = jnp.where(sub == s, b, jnp.where(sub == s + 1, area - a, two[t]))
            top, low = over_rows(rows[t], s), over_rows(rows[t], s + 1)
            for held, value in zip(kept, (left[t], right[t], rows[t])):
                held[t] = jnp.where(sub // 2 == s // 2, value, held[t])
            one_scaled = [value * scale for value in one]
            two_scaled = [value * scale for value in two]
            for k in range(j + 2, PANEL):
                x, y = over_rows(left[k // 8], k % 8), over_rows(right[k // 8], k % 8)
                for u in range(groups):
                    if k < j + 4:
                        change = (one[u] * x + two[u] * y) * scale
                    else:
                        change = one_scaled[u] * x + two_scaled[u] * y
                    columns[k][u] = columns[k][u] - change
            for u in range(groups):
                rows[u] = rows[u] - (one[u] * top + two[u] * low) * scale
            yield
        for u in range(groups):
            at = start + 8 * u
            left, right, row = (held[u] for held in kept)
            a = jnp.where(even, left, pltpu.roll(left, 1, 0))
            spread = jnp.where(even, a, a * (a * right - left * left))
            value = jnp.where(even, row, a * row - left * pltpu.roll(row, 1, 0))
            inverse[at : at + 8, :] = jnp.where(lane <= at + sub, value * lax.rsqrt(spread), 0.0)
        for g in near:
            change = tree_sum([below[g][j] * over_rows(rows[j // 8], j % 8) for j in range(PANEL)])
            tiles[g] = jnp.where(inside, 0.0, tiles[g]) - change
        if near and near[-1] + 1 < count:
            far = near[-1] + 1
            high, low = split(jnp.concatenate(rows, axis=0))
            before = [jnp.zeros((start, BLOCK), jnp.bfloat16)] * (start > 0)
            behind = [jnp.zeros((BLOCK - start - PANEL, BLOCK), jnp.bfloat16)]
            change = product(
                split(jnp.concatenate(tiles[far:], axis=0)),
                [jnp.concatenate(before + [part] + behind, axis=0) for part in (high, low)],
            )
            for i, g in enumerate(range(far, count)):
                tiles[g] = jnp.where(inside, 0.0, tiles[g]) - change[8 * i : 8 * i + 8, :]


def features(sites, left):
    x, y, z = sites[0:1, :], sites[1:2, :], 2.0 * sites[2:3, :]
    norm = x * x + y * y + z * z
    coarse = jnp.floor(norm * (1.0 / 64.0)) * 64.0
    fine = norm - coarse
    one = jnp.ones_like(x)
    if left:
        parts = (-2.0 * x, -2.0 * y, -2.0 * z, one, one, coarse, fine, 0.0 * one)
    else:
        parts = (x, y, z, coarse, fine, one, one, 0.0 * one)
    return jnp.concatenate(parts, axis=0)


def times(left, right, precision=HIGH):
    return jnp.dot(left, right, precision=precision, preferred_element_type=jnp.float32)


def product(left, right):
    return times(left[0], right[0], None) + (times(left[0], right[1], None) + times(left[1], right[0], None))


def deep_left(value):
    high, low = split(value)
    return jnp.concatenate([high, high, low], axis=1)


def deep_right(value):
    high, low = split(value)
    return jnp.concatenate([high, low, high], axis=0)


def matern(left, right):
    squared = times(left, right, None)
    root = squared * lax.rsqrt(jnp.maximum(squared, 1e-30))
    return (1.0 + inv_length * root) * jnp.exp2((-inv_length * log2_e) * root)


def split(value):
    high = value.astype(jnp.bfloat16)
    return high, (value - high.astype(jnp.float32)).astype(jnp.bfloat16)


def pack(cells, scale, packed):
    for axis in range(3):
        packed[axis : axis + 1, :] = cells[axis].astype(jnp.float32)
    packed[3:4, :] = scale[...]


def kernel(n_col, share, n_sites, panel, *refs):
    arrived = refs[:n_sites]
    lower_out, update_out, lower, update, sent, block, work, rest, left3, solved, factors, inverses, corner, scales, found, sites = refs[n_sites:]
    width = sites.shape[2]
    tiles = update.shape[1]
    count = width // BLOCK
    half = width // 2
    pivot, my_row, my_col = panel[0], lax.axis_index("row"), lax.axis_index("col")
    ids = [my_row] + [m * n_col + my_col for m in range(tiles)]
    if n_sites == 1:
        sites[...] = arrived[0][...]
        found_at = lambda i: i
    else:
        for i in range(n_sites):
            sites[i] = arrived[i][...]
        found_at = lambda i: i ^ my_row
    piv = sites[found_at(pivot)]
    blocks = [sites[found_at(i)] for i in ids]
    found[0] = features(piv, True).T
    found[1] = features(blocks[0], True).T
    rights = [features(b, False) for b in [piv] + blocks]
    for i, right in enumerate(rights):
        corner[i] = right

    def at(k):
        return slice(k * BLOCK, (k + 1) * BLOCK)

    def nuggets(row, col, shape, amount):
        same = iota(shape, 0) + row == iota(shape, 1) + col
        return jnp.where(same, amount, 0.0)

    def pivot_tile(i, j):
        value = matern(found[0, at(i), :], corner[0, :, at(j)])
        block[at(i), at(j)] = value + nuggets(0, 0, value.shape, nugget) if i == j else value

    wide = 2 * BLOCK
    pieces = width // wide

    def covariance(side, i, slot, piece, is_same):
        cols = slice(piece * wide, (piece + 1) * wide)
        value = matern(found[side, at(i), :], corner[1 + slot, :, cols])
        if piece * wide <= i * BLOCK < (piece + 1) * wide:
            value = value + nuggets(i * BLOCK, piece * wide, value.shape, jnp.where(is_same, nugget, 0.0))
        return value

    def panel_tile(i, slot, piece):
        cols = slice(slot * width + piece * wide, slot * width + (piece + 1) * wide)
        work[at(i), cols] = covariance(0, i, slot, piece, ids[slot] == pivot)

    def rest_tile(i, m, piece):
        cols = slice(m * width + piece * wide, m * width + (piece + 1) * wide)
        rest[at(i), cols] = covariance(1, i, 1 + m, piece, ids[1 + m] == my_row)

    def row_scale():
        scales[...] = jnp.broadcast_to(jnp.broadcast_to(blocks[0][3:4, :], (8, width)).T[:, 0:1], scales.shape)

    def solve(k, size, cols, factor):
        rows = slice(k * BLOCK, k * BLOCK + size)
        value = times(factor[...], deep_right(work[rows, cols]), None)
        if cols.start < width:
            work[rows, cols] = value
        for part, place_at in zip(split(value), ((0, 2 * half), (half,))):
            for start in place_at:
                start += k % 2 * BLOCK
                solved[k // 2, start : start + size, cols] = part

    def subtract(rows, cols, h, factor):
        left = factor[...]
        size = left.shape[1] // 3
        parts = [solved[h, start : start + size, cols] for start in (0, half, 2 * half)]
        work[rows, cols] = work[rows, cols] - times(left, jnp.concatenate(parts, axis=0), None)

    def keep_left(h, k):
        high, low = split(work[at(k), 0:width].T)
        j = k % 2 * BLOCK
        for place_at, part in ((0, high), (half, high), (2 * half, low)):
            left3[h, :, place_at + j : place_at + j + BLOCK] = part

    def reduce(h, rows, cols):
        return rest[rows, cols] - times(left3[h, rows, :], solved[h, :, slice(width + cols.start, width + cols.stop)], None)

    def first_half(rows, cols):
        rest[rows, cols] = reduce(0, rows, cols)

    def todo(task, *given):
        return functools.partial(task, *given)

    everything = work.shape[1]
    strips = [slice(c, c + wide) for c in range(0, everything, wide)]
    out_strips = [slice(c, c + wide) for c in range(0, tiles * width, wide)]
    halves = [slice(0, half), slice(half, width)]
    couple = slice(0, 2 * BLOCK)
    later = slice(2 * BLOCK, 4 * BLOCK)

    shadows = [[] for _ in range(count)]
    shadows[0] += [todo(pivot_tile, i, j) for i in range(count) for j in range(i, count) if i + j]
    shadows[0] += [todo(panel_tile, i, s, p) for i in range(2) for s in range(1 + tiles) for p in range(pieces)]
    shadows[0] += [row_scale]
    shadows[1] += [todo(panel_tile, i, s, p) for i in range(2, count) for s in range(1 + tiles) for p in range(pieces)]
    rest_tiles = [todo(rest_tile, i, m, p) for i in range(count) for m in range(tiles) for p in range(pieces)]
    shadows[1] += rest_tiles[: len(rest_tiles) // 2]
    shadows[2] += [todo(solve, 0, half, c, factors.at[0]) for c in strips]
    shadows[2] += [todo(subtract, later, c, 0, factors.at[1]) for c in strips]
    shadows[2] += rest_tiles[len(rest_tiles) // 2 :]
    shadows[2] += [todo(keep_left, 0, k) for k in range(2)]
    shadows[3] += [todo(solve, 2, BLOCK, c, factors.at[2, 0:BLOCK, 0 : 3 * BLOCK]) for c in strips]
    shadows[3] += [todo(subtract, at(3), c, 1, factors.at[3, 0:BLOCK, 0 : 3 * BLOCK]) for c in strips]
    shadows[3] += [todo(keep_left, 1, 2)]
    shadows[3] += [todo(first_half, r, c) for c in out_strips for r in halves]

    pivot_tile(0, 0)
    steps = BLOCK // 2
    for k in range(count):
        inverse = inverses.at[k]
        tasks = shadows[k]
        given = 0
        for step, _ in enumerate(
            eliminate([block[k * BLOCK + 8 * g : k * BLOCK + 8 * g + 8, at(k)] for g in range(BLOCK // 8)], inverse)
        ):
            goal = len(tasks) * (step + 1) // steps
            for task in tasks[given:goal]:
                task()
            given = goal
        after = slice((k + 1) * BLOCK, width)
        if k + 1 < count:
            panel = times(inverse[...], block[at(k), after])
            block[at(k), after] = panel
            for i in range(k + 1, count):
                cols = slice(i * BLOCK, width)
                here = slice((i - k - 1) * BLOCK, (i - k) * BLOCK)
                block[at(i), cols] = block[at(i), cols] - times(panel[:, here].T, panel[:, (i - k - 1) * BLOCK :])
        if k == 1:
            across = times(inverse[...], times(block[at(0), at(1)].T, inverses[0]))
            upper = jnp.concatenate([inverses[0], jnp.zeros((BLOCK, BLOCK), jnp.float32)], axis=1)
            whole = jnp.concatenate([upper, jnp.concatenate([-across, inverse[...]], axis=1)], axis=0)
            factors[0] = deep_left(whole)
            factors[1] = deep_left(block[couple, later].T)
        if k == 2:
            factors[2, 0:BLOCK, 0 : 3 * BLOCK] = deep_left(inverse[...])
            factors[3, 0:BLOCK, 0 : 3 * BLOCK] = deep_left(block[at(2), at(3)].T)
    factors[4, 0:BLOCK, 0 : 3 * BLOCK] = deep_left(inverses[3])
    for c in strips:
        solve(3, BLOCK, c, factors.at[4, 0:BLOCK, 0 : 3 * BLOCK])
    keep_left(1, 3)
    if share % BLOCK == 0:
        start = pl.multiple_of(my_col * share, BLOCK)
        lower[...] = work[pl.ds(start, share), 0:width].T * jnp.concatenate([scales[...]] * (share // BLOCK), axis=1)
    else:
        lower[...] = work[:, 0:width].T * jnp.concatenate([scales[...]] * count, axis=1)
    copies = [pltpu.make_async_copy(lower, lower_out, sent.at[0])]
    copies[0].start()
    part = BLOCK // tiles
    order = iota((BLOCK, BLOCK), 0) // tiles + iota((BLOCK, BLOCK), 0) % tiles * part
    weave = (order == iota((BLOCK, BLOCK), 1)).astype(jnp.bfloat16)
    for c in out_strips[: width // wide]:
        for r in halves:
            by_row = jnp.concatenate([scales[r, :]] * (wide // BLOCK), axis=1)
            values = []
            for m in range(tiles):
                value = reduce(1, r, slice(m * width + c.start, m * width + c.stop))
                values.append((value * by_row * blocks[1 + m][3:4, c]).astype(jnp.bfloat16))
            for row in range(0, half, part):
                stacked = jnp.concatenate([value[row : row + part, :] for value in values], axis=0)
                woven = times(weave, stacked, None).astype(jnp.bfloat16)
                update[r.start + row : r.start + row + part, :, c] = woven.reshape(part, tiles, wide)
            copies.append(pltpu.make_async_copy(update.at[r, :, c], update_out.at[r, :, c], sent.at[len(copies)]))
            copies[-1].start()
    for copy in copies:
        copy.wait()


def swap(value, step, count):
    return lax.ppermute(value, "row", [(i, i ^ step) for i in range(count)])


def on_device(site_cells, site_scale, panel):
    width = site_cells.shape[2]
    n_row = lax.axis_size("row")
    n_col = lax.axis_size("col")
    tiles = n_row // n_col
    share = width // n_col
    vmem = pl.BlockSpec(memory_space=pltpu.VMEM)
    packed = pl.pallas_call(
        pack,
        out_shape=pltpu.VMEM((4, width), jnp.float32),
        in_specs=[vmem, vmem],
        out_specs=vmem,
    )(site_cells, site_scale)
    if n_row == 8:
        arrived = [packed] + [swap(packed, k, n_row) for k in range(2, n_row, 2)]
        others = [swap(value, 1, n_row) for value in arrived]
        arrived = [value for both in zip(arrived, others) for value in both]
    else:
        arrived = [lax.all_gather(packed, "row", axis=0)]
    held = share if share % BLOCK == 0 else width
    lower, update = pl.pallas_call(
        functools.partial(kernel, n_col, share, len(arrived)),
        out_shape=(
            jax.ShapeDtypeStruct((width, held), jnp.float32),
            jax.ShapeDtypeStruct((width, tiles, width), jnp.bfloat16),
        ),
        in_specs=[pl.BlockSpec(memory_space=pltpu.SMEM)] + [vmem] * len(arrived),
        out_specs=(pl.BlockSpec(memory_space=pl.ANY),) * 2,
        scratch_shapes=[
            pltpu.VMEM((width, held), jnp.float32),
            pltpu.VMEM((width, tiles, width), jnp.bfloat16),
            pltpu.SemaphoreType.DMA((1 + width // BLOCK,)),
            pltpu.VMEM((width, width), jnp.float32),
            pltpu.VMEM((width, (1 + tiles) * width), jnp.float32),
            pltpu.VMEM((width, tiles * width), jnp.float32),
            pltpu.VMEM((2, width, 3 * width // 2), jnp.bfloat16),
            pltpu.VMEM((2, 3 * width // 2, (1 + tiles) * width), jnp.bfloat16),
            pltpu.VMEM((5, 2 * BLOCK, 6 * BLOCK), jnp.bfloat16),
            pltpu.VMEM((4, BLOCK, BLOCK), jnp.float32),
            pltpu.VMEM((2 + tiles, 8, width), jnp.float32),
            pltpu.VMEM((width, BLOCK), jnp.float32),
            pltpu.VMEM((2, width, 8), jnp.float32),
            pltpu.VMEM((n_row, 4, width), jnp.float32),
        ],
        compiler_params=pltpu.CompilerParams(vmem_limit_bytes=40 * 2**20),
    )(panel, *arrived)
    if held != share:
        lower = lax.dynamic_slice_in_dim(lower, lax.axis_index("col") * share, share, 1)
    return lower[None], update[None]


def solution(mesh):
    placed = (P(None, None, "row"), P(None, "row"), P())
    return jax.shard_map(
        on_device,
        mesh=mesh,
        in_specs=placed,
        out_specs=(P(None, "row", "col"), P(None, "row", None, "col")),
        check_vma=False,
    )
```

```python
import functools

import jax
import jax.numpy as jnp
from jax import lax
from jax.experimental import pallas as pl
from jax.experimental.pallas import tpu as pltpu
from jax.sharding import PartitionSpec as P

nugget = 0.25
inv_length = 1.7320508075688772 / 12.0
log2_e = 1.4426950408889634
BLOCK = 128
PANEL = 16
HIGH = lax.Precision.HIGH


def iota(shape, axis):
    return lax.broadcasted_iota(jnp.int32, shape, axis)


def over_rows(tile, row):
    return jnp.broadcast_to(tile[row : row + 1, :], tile.shape)


def over_lanes(tile, lane):
    return jnp.broadcast_to(tile[:, lane : lane + 1], tile.shape)


def tree_sum(parts):
    while len(parts) > 1:
        parts = [a + b for a, b in zip(parts[0::2], parts[1::2])]
    return parts[0]


def eliminate(tiles, inverse):
    tiles = list(tiles)
    count = len(tiles)
    groups = PANEL // 8
    lane = iota((8, BLOCK), 1)
    sub = iota((8, BLOCK), 0)
    even = sub % 2 == 0
    unit = [(sub == s).astype(jnp.float32) for s in range(8)]
    nothing = jnp.zeros((8, BLOCK), jnp.float32)
    for panel in range(BLOCK // PANEL):
        first = panel * groups
        start = panel * PANEL
        inside = (lane >= start) & (lane < start + PANEL)
        columns = [[over_lanes(tiles[first + u], start + j) for u in range(groups)] for j in range(PANEL)]
        rows = [
            jnp.where(inside, (lane == start + 8 * u + sub).astype(jnp.float32), tiles[first + u])
            for u in range(groups)
        ]
        near = range(first + groups, min(count, first + 2 * groups))
        below = {g: [over_lanes(tiles[g], start + j) for j in range(PANEL)] for g in near}
        kept = [[nothing] * groups for _ in range(3)]
        for j in range(0, PANEL, 2):
            t, s = divmod(j, 8)
            left, right = columns[j], columns[j + 1]
            a, b, d = over_rows(left[t], s), over_rows(right[t], s), over_rows(right[t], s + 1)
            area = a * d - b * b
            scale = 1.0 / area
            less = list(zip(left, right))
            less[t] = (left[t] - unit[s], right[t] - unit[s + 1])
            one = [x * d - y * b for x, y in less]
            two = [y * a - x * b for x, y in less]
            top, low = over_rows(rows[t], s), over_rows(rows[t], s + 1)
            for held, value in zip(kept, (left[t], right[t], rows[t])):
                held[t] = jnp.where(sub // 2 == s // 2, value, held[t])
            one_scaled = [value * scale for value in one]
            two_scaled = [value * scale for value in two]
            for k in range(j + 2, PANEL):
                x, y = over_rows(left[k // 8], k % 8), over_rows(right[k // 8], k % 8)
                for u in range(groups):
                    if k < j + 4:
                        change = (one[u] * x + two[u] * y) * scale
                    else:
                        change = one_scaled[u] * x + two_scaled[u] * y
                    columns[k][u] = columns[k][u] - change
            for u in range(groups):
                rows[u] = rows[u] - (one[u] * top + two[u] * low) * scale
            yield
        for u in range(groups):
            at = start + 8 * u
            left, right, row = (held[u] for held in kept)
            a = jnp.where(even, left, pltpu.roll(left, 1, 0))
            spread = jnp.where(even, a, a * (a * right - left * left))
            value = jnp.where(even, row, a * row - left * pltpu.roll(row, 1, 0))
            inverse[at : at + 8, :] = jnp.where(lane <= at + sub, value * lax.rsqrt(spread), 0.0)
        for g in near:
            change = tree_sum([below[g][j] * over_rows(rows[j // 8], j % 8) for j in range(PANEL)])
            tiles[g] = jnp.where(inside, 0.0, tiles[g]) - change
        if near and near[-1] + 1 < count:
            far = near[-1] + 1
            high, low = split(jnp.concatenate(rows, axis=0))
            before = [jnp.zeros((start, BLOCK), jnp.bfloat16)] * (start > 0)
            behind = [jnp.zeros((BLOCK - start - PANEL, BLOCK), jnp.bfloat16)]
            change = product(
                split(jnp.concatenate(tiles[far:], axis=0)),
                [jnp.concatenate(before + [part] + behind, axis=0) for part in (high, low)],
            )
            for i, g in enumerate(range(far, count)):
                tiles[g] = jnp.where(inside, 0.0, tiles[g]) - change[8 * i : 8 * i + 8, :]


def features(sites, left):
    x, y, z = sites[0:1, :], sites[1:2, :], 2.0 * sites[2:3, :]
    norm = x * x + y * y + z * z
    coarse = jnp.floor(norm * (1.0 / 64.0)) * 64.0
    fine = norm - coarse
    one = jnp.ones_like(x)
    if left:
        parts = (-2.0 * x, -2.0 * y, -2.0 * z, one, one, coarse, fine, 0.0 * one)
    else:
        parts = (x, y, z, coarse, fine, one, one, 0.0 * one)
    return jnp.concatenate(parts, axis=0)


def times(left, right, precision=HIGH):
    return jnp.dot(left, right, precision=precision, preferred_element_type=jnp.float32)


def product(left, right):
    return times(left[0], right[0], None) + (times(left[0], right[1], None) + times(left[1], right[0], None))


def product_turned(left, right):
    def one(a, b):
        return lax.dot_general(a, b, (((1,), (1,)), ((), ())), preferred_element_type=jnp.float32)

    return one(left[0], right[0]) + (one(left[0], right[1]) + one(left[1], right[0]))


def deep_left(value):
    high, low = split(value)
    return jnp.concatenate([high, high, low], axis=1)


def deep_right(value):
    high, low = split(value)
    return jnp.concatenate([high, low, high], axis=0)


def matern(left, right):
    squared = times(left, right, None)
    root = squared * lax.rsqrt(jnp.maximum(squared, 1e-30))
    return (1.0 + inv_length * root) * jnp.exp2((-inv_length * log2_e) * root)


def split(value):
    high = value.astype(jnp.bfloat16)
    return high, (value - high.astype(jnp.float32)).astype(jnp.bfloat16)


def pack(cells, scale, packed):
    for axis in range(3):
        packed[axis : axis + 1, :] = cells[axis].astype(jnp.float32)
    packed[3:4, :] = scale[...]


def kernel(n_col, share, n_sites, panel, *refs):
    arrived = refs[:n_sites]
    lower_out, update_out, lower, update, sent, block, work, rest, left3, solved, factors, inverses, corner, scales, found, sites = refs[n_sites:]
    width = sites.shape[2]
    tiles = update.shape[1]
    count = width // BLOCK
    half = width // 2
    pivot, my_row, my_col = panel[0], lax.axis_index("row"), lax.axis_index("col")
    ids = [my_row] + [m * n_col + my_col for m in range(tiles)]
    if n_sites == 1:
        sites[...] = arrived[0][...]
        found_at = lambda i: i
    else:
        for i in range(n_sites):
            sites[i] = arrived[i][...]
        found_at = lambda i: i ^ my_row
    piv = sites[found_at(pivot)]
    blocks = [sites[found_at(i)] for i in ids]
    found[0] = features(piv, True).T
    found[1] = features(blocks[0], True).T
    rights = [features(b, False) for b in [piv] + blocks]
    for i, right in enumerate(rights):
        corner[i] = right

    def at(k):
        return slice(k * BLOCK, (k + 1) * BLOCK)

    def nuggets(row, col, shape, amount):
        same = iota(shape, 0) + row == iota(shape, 1) + col
        return jnp.where(same, amount, 0.0)

    def pivot_tile(i, j):
        value = matern(found[0, at(i), :], corner[0, :, at(j)])
        block[at(i), at(j)] = value + nuggets(0, 0, value.shape, nugget) if i == j else value

    wide = 2 * BLOCK
    pieces = width // wide

    def covariance(side, i, slot, piece, is_same):
        cols = slice(piece * wide, (piece + 1) * wide)
        value = matern(found[side, at(i), :], corner[1 + slot, :, cols])
        if piece * wide <= i * BLOCK < (piece + 1) * wide:
            value = value + nuggets(i * BLOCK, piece * wide, value.shape, jnp.where(is_same, nugget, 0.0))
        return value

    def panel_tile(i, slot, piece):
        cols = slice(slot * width + piece * wide, slot * width + (piece + 1) * wide)
        work[at(i), cols] = covariance(0, i, slot, piece, ids[slot] == pivot)

    def rest_tile(i, m, piece):
        cols = slice(m * width + piece * wide, m * width + (piece + 1) * wide)
        rest[at(i), cols] = covariance(1, i, 1 + m, piece, ids[1 + m] == my_row)

    def row_scale():
        scales[...] = jnp.broadcast_to(jnp.broadcast_to(blocks[0][3:4, :], (8, width)).T[:, 0:1], scales.shape)

    def solve(k, size, cols, factor):
        rows = slice(k * BLOCK, k * BLOCK + size)
        value = times(factor[...], deep_right(work[rows, cols]), None)
        if cols.start < width:
            work[rows, cols] = value
        for part, place_at in zip(split(value), ((0, 2 * half), (half,))):
            for start in place_at:
                start += k % 2 * BLOCK
                solved[k // 2, start : start + size, cols] = part

    def subtract(rows, cols, h, factor):
        left = factor[...]
        size = left.shape[1] // 3
        parts = [solved[h, start : start + size, cols] for start in (0, half, 2 * half)]
        work[rows, cols] = work[rows, cols] - times(left, jnp.concatenate(parts, axis=0), None)

    def keep_left(h, k):
        high, low = split(work[at(k), 0:width].T)
        j = k % 2 * BLOCK
        for place_at, part in ((0, high), (half, high), (2 * half, low)):
            left3[h, :, place_at + j : place_at + j + BLOCK] = part

    def reduce(h, rows, cols):
        return rest[rows, cols] - times(left3[h, rows, :], solved[h, :, slice(width + cols.start, width + cols.stop)], None)

    def first_half(rows, cols):
        rest[rows, cols] = reduce(0, rows, cols)

    def todo(task, *given):
        return functools.partial(task, *given)

    everything = work.shape[1]
    strips = [slice(c, c + wide) for c in range(0, everything, wide)]
    out_strips = [slice(c, c + wide) for c in range(0, tiles * width, wide)]
    halves = [slice(0, half), slice(half, width)]
    couple = slice(0, 2 * BLOCK)
    later = slice(2 * BLOCK, 4 * BLOCK)

    shadows = [[] for _ in range(count)]
    shadows[0] += [todo(pivot_tile, i, j) for i in range(count) for j in range(i, count) if i + j]
    shadows[0] += [todo(panel_tile, i, s, p) for i in range(2) for s in range(1 + tiles) for p in range(pieces)]
    shadows[0] += [row_scale]
    shadows[1] += [todo(panel_tile, i, s, p) for i in range(2, count) for s in range(1 + tiles) for p in range(pieces)]
    rest_tiles = [todo(rest_tile, i, m, p) for i in range(count) for m in range(tiles) for p in range(pieces)]
    shadows[0] += rest_tiles[: len(rest_tiles) // 2]
    shadows[1] += rest_tiles[len(rest_tiles) // 2 :]
    shadows[2] += [todo(solve, 0, half, c, factors.at[0]) for c in strips]
    shadows[2] += [todo(subtract, later, c, 0, factors.at[1]) for c in strips]
    shadows[2] += [todo(keep_left, 0, k) for k in range(2)]
    shadows[3] += [todo(solve, 2, BLOCK, c, factors.at[2, 0:BLOCK, 0 : 3 * BLOCK]) for c in strips]
    shadows[3] += [todo(subtract, at(3), c, 1, factors.at[3, 0:BLOCK, 0 : 3 * BLOCK]) for c in strips]
    shadows[3] += [todo(keep_left, 1, 2)]
    shadows[3] += [todo(first_half, r, c) for c in out_strips for r in halves]

    pivot_tile(0, 0)
    steps = BLOCK // 2
    for k in range(count):
        inverse = inverses.at[k]
        tasks = shadows[k]
        after = slice((k + 1) * BLOCK, width)
        given = 0
        for step, _ in enumerate(
            eliminate([block[k * BLOCK + 8 * g : k * BLOCK + 8 * g + 8, at(k)] for g in range(BLOCK // 8)], inverse)
        ):
            goal = len(tasks) * (step + 1) // steps
            for task in tasks[given:goal]:
                task()
            given = goal
            if step == steps // 2 and k + 1 < count:
                turned = split(block[at(k), at(k + 1)].T)
        if k + 1 < count:
            factor = split(inverse[...])
            turned = split(product_turned(turned, factor))
            panel = product(factor, split(block[at(k), after]))
            block[at(k), after] = panel
            panels = split(panel)
            for i in range(k + 1, count):
                cols = slice(i * BLOCK, width)
                here = slice((i - k - 1) * BLOCK, (i - k) * BLOCK)
                if i > k + 1:
                    turned = split(panel[:, here].T)
                change = product(turned, [part[:, (i - k - 1) * BLOCK :] for part in panels])
                block[at(i), cols] = block[at(i), cols] - change
        if k == 1:
            across = times(inverse[...], times(block[at(0), at(1)].T, inverses[0]))
            upper = jnp.concatenate([inverses[0], jnp.zeros((BLOCK, BLOCK), jnp.float32)], axis=1)
            whole = jnp.concatenate([upper, jnp.concatenate([-across, inverse[...]], axis=1)], axis=0)
            factors[0] = deep_left(whole)
            factors[1] = deep_left(block[couple, later].T)
        if k == 2:
            factors[2, 0:BLOCK, 0 : 3 * BLOCK] = deep_left(inverse[...])
            factors[3, 0:BLOCK, 0 : 3 * BLOCK] = deep_left(block[at(2), at(3)].T)
    factors[4, 0:BLOCK, 0 : 3 * BLOCK] = deep_left(inverses[3])
    for c in strips:
        solve(3, BLOCK, c, factors.at[4, 0:BLOCK, 0 : 3 * BLOCK])
    keep_left(1, 3)
    if share % BLOCK == 0:
        start = pl.multiple_of(my_col * share, BLOCK)
        lower[...] = work[pl.ds(start, share), 0:width].T * jnp.concatenate([scales[...]] * (share // BLOCK), axis=1)
    else:
        lower[...] = work[:, 0:width].T * jnp.concatenate([scales[...]] * count, axis=1)
    copies = [pltpu.make_async_copy(lower, lower_out, sent.at[0])]
    copies[0].start()
    part = BLOCK // tiles
    order = iota((BLOCK, BLOCK), 0) // tiles + iota((BLOCK, BLOCK), 0) % tiles * part
    weave = (order == iota((BLOCK, BLOCK), 1)).astype(jnp.bfloat16)
    for c in out_strips[: width // wide]:
        for r in halves:
            by_row = jnp.concatenate([scales[r, :]] * (wide // BLOCK), axis=1)
            values = []
            for m in range(tiles):
                value = reduce(1, r, slice(m * width + c.start, m * width + c.stop))
                values.append((value * by_row * blocks[1 + m][3:4, c]).astype(jnp.bfloat16))
            for row in range(0, half, part):
                stacked = jnp.concatenate([value[row : row + part, :] for value in values], axis=0)
                woven = times(weave, stacked, None).astype(jnp.bfloat16)
                update[r.start + row : r.start + row + part, :, c] = woven.reshape(part, tiles, wide)
            copies.append(pltpu.make_async_copy(update.at[r, :, c], update_out.at[r, :, c], sent.at[len(copies)]))
            copies[-1].start()
    for copy in copies:
        copy.wait()


def swap(value, step, count):
    return lax.ppermute(value, "row", [(i, i ^ step) for i in range(count)])


def on_device(site_cells, site_scale, panel):
    width = site_cells.shape[2]
    n_row = lax.axis_size("row")
    n_col = lax.axis_size("col")
    tiles = n_row // n_col
    share = width // n_col
    vmem = pl.BlockSpec(memory_space=pltpu.VMEM)
    packed = pl.pallas_call(
        pack,
        out_shape=pltpu.VMEM((4, width), jnp.float32),
        in_specs=[vmem, vmem],
        out_specs=vmem,
    )(site_cells, site_scale)
    if n_row == 8:
        arrived = [packed] + [swap(packed, k, n_row) for k in range(2, n_row, 2)]
        others = [swap(value, 1, n_row) for value in arrived]
        arrived = [value for both in zip(arrived, others) for value in both]
    else:
        arrived = [lax.all_gather(packed, "row", axis=0)]
    held = share if share % BLOCK == 0 else width
    lower, update = pl.pallas_call(
        functools.partial(kernel, n_col, share, len(arrived)),
        out_shape=(
            jax.ShapeDtypeStruct((width, held), jnp.float32),
            jax.ShapeDtypeStruct((width, tiles, width), jnp.bfloat16),
        ),
        in_specs=[pl.BlockSpec(memory_space=pltpu.SMEM)] + [vmem] * len(arrived),
        out_specs=(pl.BlockSpec(memory_space=pl.ANY),) * 2,
        scratch_shapes=[
            pltpu.VMEM((width, held), jnp.float32),
            pltpu.VMEM((width, tiles, width), jnp.bfloat16),
            pltpu.SemaphoreType.DMA((1 + width // BLOCK,)),
            pltpu.VMEM((width, width), jnp.float32),
            pltpu.VMEM((width, (1 + tiles) * width), jnp.float32),
            pltpu.VMEM((width, tiles * width), jnp.float32),
            pltpu.VMEM((2, width, 3 * width // 2), jnp.bfloat16),
            pltpu.VMEM((2, 3 * width // 2, (1 + tiles) * width), jnp.bfloat16),
            pltpu.VMEM((5, 2 * BLOCK, 6 * BLOCK), jnp.bfloat16),
            pltpu.VMEM((4, BLOCK, BLOCK), jnp.float32),
            pltpu.VMEM((2 + tiles, 8, width), jnp.float32),
            pltpu.VMEM((width, BLOCK), jnp.float32),
            pltpu.VMEM((2, width, 8), jnp.float32),
            pltpu.VMEM((n_row, 4, width), jnp.float32),
        ],
        compiler_params=pltpu.CompilerParams(vmem_limit_bytes=40 * 2**20),
    )(panel, *arrived)
    if held != share:
        lower = lax.dynamic_slice_in_dim(lower, lax.axis_index("col") * share, share, 1)
    return lower[None], update[None]


def solution(mesh):
    placed = (P(None, None, "row"), P(None, "row"), P())
    return jax.shard_map(
        on_device,
        mesh=mesh,
        in_specs=placed,
        out_specs=(P(None, "row", "col"), P(None, "row", None, "col")),
        check_vma=False,
    )
```

```python
import functools

import jax
import jax.numpy as jnp
from jax import lax
from jax.experimental import pallas as pl
from jax.experimental.pallas import tpu as pltpu
from jax.sharding import PartitionSpec as P

nugget = 0.25
inv_length = 1.7320508075688772 / 12.0
log2_e = 1.4426950408889634
BLOCK = 128
PANEL = 16
HIGH = lax.Precision.HIGH
FULL = lax.Precision.HIGHEST


def iota(shape, axis):
    return lax.broadcasted_iota(jnp.int32, shape, axis)


def over_rows(tile, row):
    return jnp.broadcast_to(tile[row : row + 1, :], tile.shape)


def over_lanes(tile, lane):
    return jnp.broadcast_to(tile[:, lane : lane + 1], tile.shape)


def tree_sum(parts):
    while len(parts) > 1:
        parts = [a + b for a, b in zip(parts[0::2], parts[1::2])]
    return parts[0]


def eliminate(tiles, inverse):
    tiles = list(tiles)
    count = len(tiles)
    groups = PANEL // 8
    lane = iota((8, BLOCK), 1)
    sub = iota((8, BLOCK), 0)
    even = sub % 2 == 0
    unit = [(sub == s).astype(jnp.float32) for s in range(8)]
    nothing = jnp.zeros((8, BLOCK), jnp.float32)
    for panel in range(BLOCK // PANEL):
        first = panel * groups
        start = panel * PANEL
        inside = (lane >= start) & (lane < start + PANEL)
        columns = [[over_lanes(tiles[first + u], start + j) for u in range(groups)] for j in range(PANEL)]
        rows = [
            jnp.where(inside, (lane == start + 8 * u + sub).astype(jnp.float32), tiles[first + u])
            for u in range(groups)
        ]
        near = range(first + groups, min(count, first + 2 * groups))
        below = {g: [over_lanes(tiles[g], start + j) for j in range(PANEL)] for g in near}
        kept = [[nothing] * groups for _ in range(3)]
        for j in range(0, PANEL, 2):
            t, s = divmod(j, 8)
            left, right = columns[j], columns[j + 1]
            a, b, d = over_rows(left[t], s), over_rows(right[t], s), over_rows(right[t], s + 1)
            area = a * d - b * b
            scale = 1.0 / area
            less = list(zip(left, right))
            less[t] = (left[t] - unit[s], right[t] - unit[s + 1])
            one = [x * d - y * b for x, y in less]
            two = [y * a - x * b for x, y in less]
            top, low = over_rows(rows[t], s), over_rows(rows[t], s + 1)
            for held, value in zip(kept, (left[t], right[t], rows[t])):
                held[t] = jnp.where(sub // 2 == s // 2, value, held[t])
            one_scaled = [value * scale for value in one]
            two_scaled = [value * scale for value in two]
            for k in range(j + 2, PANEL):
                x, y = over_rows(left[k // 8], k % 8), over_rows(right[k // 8], k % 8)
                for u in range(groups):
                    if k < j + 4:
                        change = (one[u] * x + two[u] * y) * scale
                    else:
                        change = one_scaled[u] * x + two_scaled[u] * y
                    columns[k][u] = columns[k][u] - change
            for u in range(groups):
                rows[u] = rows[u] - (one[u] * top + two[u] * low) * scale
            yield
        for u in range(groups):
            at = start + 8 * u
            left, right, row = (held[u] for held in kept)
            a = jnp.where(even, left, pltpu.roll(left, 1, 0))
            spread = jnp.where(even, a, a * (a * right - left * left))
            value = jnp.where(even, row, a * row - left * pltpu.roll(row, 1, 0))
            inverse[at : at + 8, :] = jnp.where(lane <= at + sub, value * lax.rsqrt(spread), 0.0)
        for g in near:
            change = tree_sum([below[g][j] * over_rows(rows[j // 8], j % 8) for j in range(PANEL)])
            tiles[g] = jnp.where(inside, 0.0, tiles[g]) - change
        if near and near[-1] + 1 < count:
            far = near[-1] + 1
            padded = jnp.concatenate([nothing] * first + rows + [nothing] * (count - first - groups), axis=0)
            change = times(jnp.concatenate(tiles[far:], axis=0), padded, FULL)
            for i, g in enumerate(range(far, count)):
                tiles[g] = jnp.where(inside, 0.0, tiles[g]) - change[8 * i : 8 * i + 8, :]


def features(sites, left):
    x, y, z = sites[0:1, :], sites[1:2, :], 2.0 * sites[2:3, :]
    norm = x * x + y * y + z * z
    coarse = jnp.floor(norm * (1.0 / 64.0)) * 64.0
    fine = norm - coarse
    one = jnp.ones_like(x)
    if left:
        parts = (-2.0 * x, -2.0 * y, -2.0 * z, one, one, coarse, fine, 0.0 * one)
    else:
        parts = (x, y, z, coarse, fine, one, one, 0.0 * one)
    return jnp.concatenate(parts, axis=0)


def times(left, right, precision=HIGH):
    return jnp.dot(left, right, precision=precision, preferred_element_type=jnp.float32)


def product(left, right):
    return times(left[0], right[0], None) + (times(left[0], right[1], None) + times(left[1], right[0], None))


def times_turned(left, right):
    return lax.dot_general(
        left, right, (((1,), (1,)), ((), ())), precision=FULL, preferred_element_type=jnp.float32
    )


def deep_left(value):
    high, low = split(value)
    return jnp.concatenate([high, high, low], axis=1)


def deep_right(value):
    high, low = split(value)
    return jnp.concatenate([high, low, high], axis=0)


def matern(left, right):
    squared = times(left, right, None)
    root = squared * lax.rsqrt(jnp.maximum(squared, 1e-30))
    return (1.0 + inv_length * root) * jnp.exp2((-inv_length * log2_e) * root)


def split(value):
    high = value.astype(jnp.bfloat16)
    return high, (value - high.astype(jnp.float32)).astype(jnp.bfloat16)


def pack(cells, scale, packed):
    for axis in range(3):
        packed[axis : axis + 1, :] = cells[axis].astype(jnp.float32)
    packed[3:4, :] = scale[...]


def kernel(n_col, share, n_sites, panel, *refs):
    arrived = refs[:n_sites]
    lower_out, update_out, lower, update, sent, block, work, rest, left3, solved, factors, inverses, corner, scales, found, sites = refs[n_sites:]
    width = sites.shape[2]
    tiles = update.shape[1]
    count = width // BLOCK
    half = width // 2
    pivot, my_row, my_col = panel[0], lax.axis_index("row"), lax.axis_index("col")
    ids = [my_row] + [m * n_col + my_col for m in range(tiles)]
    if n_sites == 1:
        sites[...] = arrived[0][...]
        found_at = lambda i: i
    else:
        for i in range(n_sites):
            sites[i] = arrived[i][...]
        found_at = lambda i: i ^ my_row
    piv = sites[found_at(pivot)]
    blocks = [sites[found_at(i)] for i in ids]
    found[0] = features(piv, True).T
    found[1] = features(blocks[0], True).T
    rights = [features(b, False) for b in [piv] + blocks]
    for i, right in enumerate(rights):
        corner[i] = right

    def at(k):
        return slice(k * BLOCK, (k + 1) * BLOCK)

    def nuggets(row, col, shape, amount):
        same = iota(shape, 0) + row == iota(shape, 1) + col
        return jnp.where(same, amount, 0.0)

    def pivot_tile(i, j):
        value = matern(found[0, at(i), :], corner[0, :, at(j)])
        block[at(i), at(j)] = value + nuggets(0, 0, value.shape, nugget) if i == j else value

    wide = 2 * BLOCK
    pieces = width // wide

    def covariance(side, i, slot, piece, is_same):
        cols = slice(piece * wide, (piece + 1) * wide)
        value = matern(found[side, at(i), :], corner[1 + slot, :, cols])
        if piece * wide <= i * BLOCK < (piece + 1) * wide:
            value = value + nuggets(i * BLOCK, piece * wide, value.shape, jnp.where(is_same, nugget, 0.0))
        return value

    def panel_tile(i, slot, piece):
        cols = slice(slot * width + piece * wide, slot * width + (piece + 1) * wide)
        work[at(i), cols] = covariance(0, i, slot, piece, ids[slot] == pivot)

    def rest_tile(i, m, piece):
        cols = slice(m * width + piece * wide, m * width + (piece + 1) * wide)
        rest[at(i), cols] = covariance(1, i, 1 + m, piece, ids[1 + m] == my_row)

    def row_scale():
        scales[...] = jnp.broadcast_to(jnp.broadcast_to(blocks[0][3:4, :], (8, width)).T[:, 0:1], scales.shape)

    def solve(k, size, cols, factor):
        rows = slice(k * BLOCK, k * BLOCK + size)
        value = times(factor[...], deep_right(work[rows, cols]), None)
        if cols.start < width:
            work[rows, cols] = value
        for part, place_at in zip(split(value), ((0, 2 * half), (half,))):
            for start in place_at:
                start += k % 2 * BLOCK
                solved[k // 2, start : start + size, cols] = part

    def subtract(rows, cols, h, factor):
        left = factor[...]
        size = left.shape[1] // 3
        parts = [solved[h, start : start + size, cols] for start in (0, half, 2 * half)]
        work[rows, cols] = work[rows, cols] - times(left, jnp.concatenate(parts, axis=0), None)

    def keep_left(h, k):
        high, low = split(work[at(k), 0:width].T)
        j = k % 2 * BLOCK
        for place_at, part in ((0, high), (half, high), (2 * half, low)):
            left3[h, :, place_at + j : place_at + j + BLOCK] = part

    def reduce(h, rows, cols):
        return rest[rows, cols] - times(left3[h, rows, :], solved[h, :, slice(width + cols.start, width + cols.stop)], None)

    def first_half(rows, cols):
        rest[rows, cols] = reduce(0, rows, cols)

    def todo(task, *given):
        return functools.partial(task, *given)

    everything = work.shape[1]
    strips = [slice(c, c + wide) for c in range(0, everything, wide)]
    out_strips = [slice(c, c + wide) for c in range(0, tiles * width, wide)]
    halves = [slice(0, half), slice(half, width)]
    couple = slice(0, 2 * BLOCK)
    later = slice(2 * BLOCK, 4 * BLOCK)

    shadows = [[] for _ in range(count)]
    shadows[0] += [todo(pivot_tile, i, j) for i in range(count) for j in range(i, count) if i + j]
    shadows[0] += [todo(panel_tile, i, s, p) for i in range(2) for s in range(1 + tiles) for p in range(pieces)]
    shadows[0] += [row_scale]
    shadows[1] += [todo(panel_tile, i, s, p) for i in range(2, count) for s in range(1 + tiles) for p in range(pieces)]
    rest_tiles = [todo(rest_tile, i, m, p) for i in range(count) for m in range(tiles) for p in range(pieces)]
    shadows[0] += rest_tiles[: len(rest_tiles) // 2]
    shadows[1] += rest_tiles[len(rest_tiles) // 2 :]
    shadows[2] += [todo(solve, 0, half, c, factors.at[0]) for c in strips]
    shadows[2] += [todo(subtract, later, c, 0, factors.at[1]) for c in strips]
    shadows[2] += [todo(keep_left, 0, k) for k in range(2)]
    shadows[3] += [todo(solve, 2, BLOCK, c, factors.at[2, 0:BLOCK, 0 : 3 * BLOCK]) for c in strips]
    shadows[3] += [todo(subtract, at(3), c, 1, factors.at[3, 0:BLOCK, 0 : 3 * BLOCK]) for c in strips]
    shadows[3] += [todo(keep_left, 1, 2)]
    shadows[3] += [todo(first_half, r, c) for c in out_strips for r in halves]

    pivot_tile(0, 0)
    steps = BLOCK // 2
    for k in range(count):
        inverse = inverses.at[k]
        tasks = shadows[k]
        after = slice((k + 1) * BLOCK, width)
        given = 0
        for step, _ in enumerate(
            eliminate([block[k * BLOCK + 8 * g : k * BLOCK + 8 * g + 8, at(k)] for g in range(BLOCK // 8)], inverse)
        ):
            goal = len(tasks) * (step + 1) // steps
            for task in tasks[given:goal]:
                task()
            given = goal
            if step == steps // 2 and k + 1 < count:
                turned = block[at(k), at(k + 1)].T
        if k + 1 < count:
            factor = inverse[...]
            turned = times_turned(turned, factor)
            panel = times(factor, block[at(k), after], FULL)
            block[at(k), after] = panel
            for i in range(k + 1, count):
                cols = slice(i * BLOCK, width)
                here = slice((i - k - 1) * BLOCK, (i - k) * BLOCK)
                if i > k + 1:
                    turned = panel[:, here].T
                change = times(turned, panel[:, (i - k - 1) * BLOCK :], FULL)
                block[at(i), cols] = block[at(i), cols] - change
        if k == 1:
            across = times(inverse[...], times(block[at(0), at(1)].T, inverses[0], FULL), FULL)
            upper = jnp.concatenate([inverses[0], jnp.zeros((BLOCK, BLOCK), jnp.float32)], axis=1)
            whole = jnp.concatenate([upper, jnp.concatenate([-across, inverse[...]], axis=1)], axis=0)
            factors[0] = deep_left(whole)
            factors[1] = deep_left(block[couple, later].T)
        if k == 2:
            factors[2, 0:BLOCK, 0 : 3 * BLOCK] = deep_left(inverse[...])
            factors[3, 0:BLOCK, 0 : 3 * BLOCK] = deep_left(block[at(2), at(3)].T)
    factors[4, 0:BLOCK, 0 : 3 * BLOCK] = deep_left(inverses[3])
    for c in strips:
        solve(3, BLOCK, c, factors.at[4, 0:BLOCK, 0 : 3 * BLOCK])
    keep_left(1, 3)
    if share % BLOCK == 0:
        start = pl.multiple_of(my_col * share, BLOCK)
        lower[...] = work[pl.ds(start, share), 0:width].T * jnp.concatenate([scales[...]] * (share // BLOCK), axis=1)
    else:
        lower[...] = work[:, 0:width].T * jnp.concatenate([scales[...]] * count, axis=1)
    copies = [pltpu.make_async_copy(lower, lower_out, sent.at[0])]
    copies[0].start()
    part = BLOCK // tiles
    order = iota((BLOCK, BLOCK), 0) // tiles + iota((BLOCK, BLOCK), 0) % tiles * part
    weave = (order == iota((BLOCK, BLOCK), 1)).astype(jnp.bfloat16)
    for c in out_strips[: width // wide]:
        for r in halves:
            by_row = jnp.concatenate([scales[r, :]] * (wide // BLOCK), axis=1)
            values = []
            for m in range(tiles):
                value = reduce(1, r, slice(m * width + c.start, m * width + c.stop))
                values.append((value * by_row * blocks[1 + m][3:4, c]).astype(jnp.bfloat16))
            for row in range(0, half, part):
                stacked = jnp.concatenate([value[row : row + part, :] for value in values], axis=0)
                woven = times(weave, stacked, None).astype(jnp.bfloat16)
                update[r.start + row : r.start + row + part, :, c] = woven.reshape(part, tiles, wide)
            copies.append(pltpu.make_async_copy(update.at[r, :, c], update_out.at[r, :, c], sent.at[len(copies)]))
            copies[-1].start()
    for copy in copies:
        copy.wait()


def swap(value, step, count):
    return lax.ppermute(value, "row", [(i, i ^ step) for i in range(count)])


def on_device(site_cells, site_scale, panel):
    width = site_cells.shape[2]
    n_row = lax.axis_size("row")
    n_col = lax.axis_size("col")
    tiles = n_row // n_col
    share = width // n_col
    vmem = pl.BlockSpec(memory_space=pltpu.VMEM)
    packed = pl.pallas_call(
        pack,
        out_shape=pltpu.VMEM((4, width), jnp.float32),
        in_specs=[vmem, vmem],
        out_specs=vmem,
    )(site_cells, site_scale)
    if n_row == 8:
        arrived = [packed] + [swap(packed, k, n_row) for k in range(2, n_row, 2)]
        others = [swap(value, 1, n_row) for value in arrived]
        arrived = [value for both in zip(arrived, others) for value in both]
    else:
        arrived = [lax.all_gather(packed, "row", axis=0)]
    held = share if share % BLOCK == 0 else width
    lower, update = pl.pallas_call(
        functools.partial(kernel, n_col, share, len(arrived)),
        out_shape=(
            jax.ShapeDtypeStruct((width, held), jnp.float32),
            jax.ShapeDtypeStruct((width, tiles, width), jnp.bfloat16),
        ),
        in_specs=[pl.BlockSpec(memory_space=pltpu.SMEM)] + [vmem] * len(arrived),
        out_specs=(pl.BlockSpec(memory_space=pl.ANY),) * 2,
        scratch_shapes=[
            pltpu.VMEM((width, held), jnp.float32),
            pltpu.VMEM((width, tiles, width), jnp.bfloat16),
            pltpu.SemaphoreType.DMA((1 + width // BLOCK,)),
            pltpu.VMEM((width, width), jnp.float32),
            pltpu.VMEM((width, (1 + tiles) * width), jnp.float32),
            pltpu.VMEM((width, tiles * width), jnp.float32),
            pltpu.VMEM((2, width, 3 * width // 2), jnp.bfloat16),
            pltpu.VMEM((2, 3 * width // 2, (1 + tiles) * width), jnp.bfloat16),
            pltpu.VMEM((5, 2 * BLOCK, 6 * BLOCK), jnp.bfloat16),
            pltpu.VMEM((4, BLOCK, BLOCK), jnp.float32),
            pltpu.VMEM((2 + tiles, 8, width), jnp.float32),
            pltpu.VMEM((width, BLOCK), jnp.float32),
            pltpu.VMEM((2, width, 8), jnp.float32),
            pltpu.VMEM((n_row, 4, width), jnp.float32),
        ],
        compiler_params=pltpu.CompilerParams(vmem_limit_bytes=40 * 2**20),
    )(panel, *arrived)
    if held != share:
        lower = lax.dynamic_slice_in_dim(lower, lax.axis_index("col") * share, share, 1)
    return lower[None], update[None]


def solution(mesh):
    placed = (P(None, None, "row"), P(None, "row"), P())
    return jax.shard_map(
        on_device,
        mesh=mesh,
        in_specs=placed,
        out_specs=(P(None, "row", "col"), P(None, "row", None, "col")),
        check_vma=False,
    )
```

```python
import functools

import jax
import jax.numpy as jnp
from jax import lax
from jax.experimental import pallas as pl
from jax.experimental.pallas import tpu as pltpu
from jax.sharding import PartitionSpec as P

nugget = 0.25
inv_length = 1.7320508075688772 / 12.0
log2_e = 1.4426950408889634
BLOCK = 128
PANEL = 16
HIGH = lax.Precision.HIGH
FULL = lax.Precision.HIGHEST


def iota(shape, axis):
    return lax.broadcasted_iota(jnp.int32, shape, axis)


def over_rows(tile, row):
    return jnp.broadcast_to(tile[row : row + 1, :], tile.shape)


def over_lanes(tile, lane):
    return jnp.broadcast_to(tile[:, lane : lane + 1], tile.shape)


def tree_sum(parts):
    while len(parts) > 1:
        parts = [a + b for a, b in zip(parts[0::2], parts[1::2])]
    return parts[0]


def eliminate(tiles, inverse):
    tiles = list(tiles)
    count = len(tiles)
    groups = PANEL // 8
    lane = iota((8, BLOCK), 1)
    sub = iota((8, BLOCK), 0)
    even = sub % 2 == 0
    unit = [(sub == s).astype(jnp.float32) for s in range(8)]
    nothing = jnp.zeros((8, BLOCK), jnp.float32)
    for panel in range(BLOCK // PANEL):
        first = panel * groups
        start = panel * PANEL
        inside = (lane >= start) & (lane < start + PANEL)
        columns = [[over_lanes(tiles[first + u], start + j) for u in range(groups)] for j in range(PANEL)]
        rows = [
            jnp.where(inside, (lane == start + 8 * u + sub).astype(jnp.float32), tiles[first + u])
            for u in range(groups)
        ]
        near = range(first + groups, min(count, first + 2 * groups))
        below = {g: [over_lanes(tiles[g], start + j) for j in range(PANEL)] for g in near}
        kept = [[nothing] * groups for _ in range(3)]
        for j in range(0, PANEL, 2):
            t, s = divmod(j, 8)
            left, right = columns[j], columns[j + 1]
            a, b, d = over_rows(left[t], s), over_rows(right[t], s), over_rows(right[t], s + 1)
            area = a * d - b * b
            scale = 1.0 / area
            less = list(zip(left, right))
            less[t] = (left[t] - unit[s], right[t] - unit[s + 1])
            one = [x * d - y * b for x, y in less]
            two = [y * a - x * b for x, y in less]
            top, low = over_rows(rows[t], s), over_rows(rows[t], s + 1)
            for held, value in zip(kept, (left[t], right[t], rows[t])):
                held[t] = jnp.where(sub // 2 == s // 2, value, held[t])
            one_scaled = [value * scale for value in one]
            two_scaled = [value * scale for value in two]
            for k in range(j + 2, PANEL):
                x, y = over_rows(left[k // 8], k % 8), over_rows(right[k // 8], k % 8)
                for u in range(groups):
                    if k < j + 4:
                        change = (one[u] * x + two[u] * y) * scale
                    else:
                        change = one_scaled[u] * x + two_scaled[u] * y
                    columns[k][u] = columns[k][u] - change
            for u in range(groups):
                rows[u] = rows[u] - (one[u] * top + two[u] * low) * scale
            yield
        for u in range(groups):
            at = start + 8 * u
            left, right, row = (held[u] for held in kept)
            a = jnp.where(even, left, pltpu.roll(left, 1, 0))
            spread = jnp.where(even, a, a * (a * right - left * left))
            value = jnp.where(even, row, a * row - left * pltpu.roll(row, 1, 0))
            inverse[at : at + 8, :] = jnp.where(lane <= at + sub, value * lax.rsqrt(spread), 0.0)
        for g in near:
            change = tree_sum([below[g][j] * over_rows(rows[j // 8], j % 8) for j in range(PANEL)])
            tiles[g] = jnp.where(inside, 0.0, tiles[g]) - change
        if near and near[-1] + 1 < count:
            far = near[-1] + 1
            padded = jnp.concatenate([nothing] * first + rows + [nothing] * (count - first - groups), axis=0)
            change = times(jnp.concatenate(tiles[far:], axis=0), padded, FULL)
            for i, g in enumerate(range(far, count)):
                tiles[g] = jnp.where(inside, 0.0, tiles[g]) - change[8 * i : 8 * i + 8, :]


def features(sites, left):
    x, y, z = sites[0:1, :], sites[1:2, :], 2.0 * sites[2:3, :]
    norm = x * x + y * y + z * z
    coarse = jnp.floor(norm * (1.0 / 64.0)) * 64.0
    fine = norm - coarse
    one = jnp.ones_like(x)
    if left:
        parts = (-2.0 * x, -2.0 * y, -2.0 * z, one, one, coarse, fine, 0.0 * one)
    else:
        parts = (x, y, z, coarse, fine, one, one, 0.0 * one)
    return jnp.concatenate(parts, axis=0)


def times(left, right, precision=HIGH):
    return jnp.dot(left, right, precision=precision, preferred_element_type=jnp.float32)


def product(left, right):
    return times(left[0], right[0], None) + (times(left[0], right[1], None) + times(left[1], right[0], None))


def times_turned(left, right):
    return lax.dot_general(
        left, right, (((1,), (1,)), ((), ())), precision=FULL, preferred_element_type=jnp.float32
    )


def deep_left(value):
    high, low = split(value)
    return jnp.concatenate([high, high, low], axis=1)


def deep_right(value):
    high, low = split(value)
    return jnp.concatenate([high, low, high], axis=0)


def matern(left, right):
    squared = times(left, right, None)
    root = squared * lax.rsqrt(jnp.maximum(squared, 1e-30))
    return (1.0 + inv_length * root) * jnp.exp2((-inv_length * log2_e) * root)


def split(value):
    high = value.astype(jnp.bfloat16)
    return high, (value - high.astype(jnp.float32)).astype(jnp.bfloat16)


def pack(cells, scale, packed):
    for axis in range(3):
        packed[axis : axis + 1, :] = cells[axis].astype(jnp.float32)
    packed[3:4, :] = scale[...]


def kernel(n_col, share, n_sites, panel, *refs):
    arrived = refs[:n_sites]
    lower_out, update_out, lower, update, sent, block, work, rest, left3, solved, factors, inverses, corner, scales, found, sites = refs[n_sites:]
    width = sites.shape[2]
    tiles = update.shape[1]
    count = width // BLOCK
    half = width // 2
    pivot, my_row, my_col = panel[0], lax.axis_index("row"), lax.axis_index("col")
    ids = [my_row] + [m * n_col + my_col for m in range(tiles)]
    if n_sites == 1:
        sites[...] = arrived[0][...]
        found_at = lambda i: i
    else:
        for i in range(n_sites):
            sites[i] = arrived[i][...]
        found_at = lambda i: i ^ my_row
    piv = sites[found_at(pivot)]
    blocks = [sites[found_at(i)] for i in ids]
    found[0] = features(piv, True).T
    found[1] = features(blocks[0], True).T
    rights = [features(b, False) for b in [piv] + blocks]
    for i, right in enumerate(rights):
        corner[i] = right

    def at(k):
        return slice(k * BLOCK, (k + 1) * BLOCK)

    def nuggets(row, col, shape, amount):
        same = iota(shape, 0) + row == iota(shape, 1) + col
        return jnp.where(same, amount, 0.0)

    def pivot_tile(i, j):
        value = matern(found[0, at(i), :], corner[0, :, at(j)])
        block[at(i), at(j)] = value + nuggets(0, 0, value.shape, nugget) if i == j else value

    wide = 2 * BLOCK
    pieces = width // wide

    def covariance(side, i, slot, piece, is_same):
        cols = slice(piece * wide, (piece + 1) * wide)
        value = matern(found[side, at(i), :], corner[1 + slot, :, cols])
        if piece * wide <= i * BLOCK < (piece + 1) * wide:
            value = value + nuggets(i * BLOCK, piece * wide, value.shape, jnp.where(is_same, nugget, 0.0))
        return value

    def panel_tile(i, slot, piece):
        cols = slice(slot * width + piece * wide, slot * width + (piece + 1) * wide)
        work[at(i), cols] = covariance(0, i, slot, piece, ids[slot] == pivot)

    def rest_tile(i, m, piece):
        cols = slice(m * width + piece * wide, m * width + (piece + 1) * wide)
        rest[at(i), cols] = covariance(1, i, 1 + m, piece, ids[1 + m] == my_row)

    def row_scale():
        scales[...] = jnp.broadcast_to(jnp.broadcast_to(blocks[0][3:4, :], (8, width)).T[:, 0:1], scales.shape)

    def solve(k, size, cols, factor):
        rows = slice(k * BLOCK, k * BLOCK + size)
        value = times(factor[...], deep_right(work[rows, cols]), None)
        if cols.start < width:
            work[rows, cols] = value
        for part, place_at in zip(split(value), ((0, 2 * half), (half,))):
            for start in place_at:
                start += k % 2 * BLOCK
                solved[k // 2, start : start + size, cols] = part

    def subtract(rows, cols, h, factor):
        left = factor[...]
        size = left.shape[1] // 3
        parts = [solved[h, start : start + size, cols] for start in (0, half, 2 * half)]
        work[rows, cols] = work[rows, cols] - times(left, jnp.concatenate(parts, axis=0), None)

    def keep_left(h, k):
        high, low = split(work[at(k), 0:width].T)
        j = k % 2 * BLOCK
        for place_at, part in ((0, high), (half, high), (2 * half, low)):
            left3[h, :, place_at + j : place_at + j + BLOCK] = part

    def one_block(k, rows, cols):
        h, j = k // 2, k % 2 * BLOCK
        pieces = [slice(start + j, start + j + BLOCK) for start in (0, half, 2 * half)]
        left = jnp.concatenate([left3[h, rows, piece] for piece in pieces], axis=1)
        right = jnp.concatenate([solved[h, piece, slice(width + cols.start, width + cols.stop)] for piece in pieces], axis=0)
        return rest[rows, cols] - times(left, right, None)

    def third_part(rows, cols):
        rest[rows, cols] = one_block(2, rows, cols)

    def reduce(h, rows, cols):
        return rest[rows, cols] - times(left3[h, rows, :], solved[h, :, slice(width + cols.start, width + cols.stop)], None)

    def first_half(rows, cols):
        rest[rows, cols] = reduce(0, rows, cols)

    def todo(task, *given):
        return functools.partial(task, *given)

    everything = work.shape[1]
    strips = [slice(c, c + wide) for c in range(0, everything, wide)]
    out_strips = [slice(c, c + wide) for c in range(0, tiles * width, wide)]
    halves = [slice(0, half), slice(half, width)]
    couple = slice(0, 2 * BLOCK)
    later = slice(2 * BLOCK, 4 * BLOCK)

    shadows = [[] for _ in range(count)]
    shadows[0] += [todo(pivot_tile, i, j) for i in range(count) for j in range(i, count) if i + j]
    shadows[0] += [todo(panel_tile, i, s, p) for i in range(2) for s in range(1 + tiles) for p in range(pieces)]
    shadows[0] += [row_scale]
    shadows[1] += [todo(panel_tile, i, s, p) for i in range(2, count) for s in range(1 + tiles) for p in range(pieces)]
    rest_tiles = [todo(rest_tile, i, m, p) for i in range(count) for m in range(tiles) for p in range(pieces)]
    shadows[0] += rest_tiles[: len(rest_tiles) // 2]
    shadows[1] += rest_tiles[len(rest_tiles) // 2 :]
    shadows[2] += [todo(solve, 0, half, c, factors.at[0]) for c in strips]
    shadows[2] += [todo(subtract, later, c, 0, factors.at[1]) for c in strips]
    shadows[2] += [todo(keep_left, 0, k) for k in range(2)]
    shadows[3] += [todo(solve, 2, BLOCK, c, factors.at[2, 0:BLOCK, 0 : 3 * BLOCK]) for c in strips]
    shadows[3] += [todo(subtract, at(3), c, 1, factors.at[3, 0:BLOCK, 0 : 3 * BLOCK]) for c in strips]
    shadows[3] += [todo(keep_left, 1, 2)]
    shadows[3] += [todo(first_half, r, c) for c in out_strips for r in halves]
    shadows[3] += [todo(third_part, r, c) for c in out_strips for r in halves]

    pivot_tile(0, 0)
    steps = BLOCK // 2
    for k in range(count):
        inverse = inverses.at[k]
        tasks = shadows[k]
        after = slice((k + 1) * BLOCK, width)
        given = 0
        for step, _ in enumerate(
            eliminate([block[k * BLOCK + 8 * g : k * BLOCK + 8 * g + 8, at(k)] for g in range(BLOCK // 8)], inverse)
        ):
            goal = len(tasks) * (step + 1) // steps
            for task in tasks[given:goal]:
                task()
            given = goal
            if step == steps // 2 and k + 1 < count:
                turned = block[at(k), at(k + 1)].T
        if k + 1 < count:
            factor = inverse[...]
            turned = times_turned(turned, factor)
            panel = times(factor, block[at(k), after], FULL)
            block[at(k), after] = panel
            for i in range(k + 1, count):
                cols = slice(i * BLOCK, width)
                here = slice((i - k - 1) * BLOCK, (i - k) * BLOCK)
                if i > k + 1:
                    turned = panel[:, here].T
                change = times(turned, panel[:, (i - k - 1) * BLOCK :], FULL)
                block[at(i), cols] = block[at(i), cols] - change
        if k == 1:
            across = times(inverse[...], times(block[at(0), at(1)].T, inverses[0], FULL), FULL)
            upper = jnp.concatenate([inverses[0], jnp.zeros((BLOCK, BLOCK), jnp.float32)], axis=1)
            whole = jnp.concatenate([upper, jnp.concatenate([-across, inverse[...]], axis=1)], axis=0)
            factors[0] = deep_left(whole)
            factors[1] = deep_left(block[couple, later].T)
        if k == 2:
            factors[2, 0:BLOCK, 0 : 3 * BLOCK] = deep_left(inverse[...])
            factors[3, 0:BLOCK, 0 : 3 * BLOCK] = deep_left(block[at(2), at(3)].T)
    factors[4, 0:BLOCK, 0 : 3 * BLOCK] = deep_left(inverses[3])
    for c in strips:
        solve(3, BLOCK, c, factors.at[4, 0:BLOCK, 0 : 3 * BLOCK])
    keep_left(1, 3)
    if share % BLOCK == 0:
        start = pl.multiple_of(my_col * share, BLOCK)
        lower[...] = work[pl.ds(start, share), 0:width].T * jnp.concatenate([scales[...]] * (share // BLOCK), axis=1)
    else:
        lower[...] = work[:, 0:width].T * jnp.concatenate([scales[...]] * count, axis=1)
    copies = [pltpu.make_async_copy(lower, lower_out, sent.at[0])]
    copies[0].start()
    part = BLOCK // tiles
    order = iota((BLOCK, BLOCK), 0) // tiles + iota((BLOCK, BLOCK), 0) % tiles * part
    weave = (order == iota((BLOCK, BLOCK), 1)).astype(jnp.bfloat16)
    for c in out_strips[: width // wide]:
        for r in halves:
            by_row = jnp.concatenate([scales[r, :]] * (wide // BLOCK), axis=1)
            values = []
            for m in range(tiles):
                value = one_block(3, r, slice(m * width + c.start, m * width + c.stop))
                values.append((value * by_row * blocks[1 + m][3:4, c]).astype(jnp.bfloat16))
            for row in range(0, half, part):
                stacked = jnp.concatenate([value[row : row + part, :] for value in values], axis=0)
                woven = times(weave, stacked, None).astype(jnp.bfloat16)
                update[r.start + row : r.start + row + part, :, c] = woven.reshape(part, tiles, wide)
            copies.append(pltpu.make_async_copy(update.at[r, :, c], update_out.at[r, :, c], sent.at[len(copies)]))
            copies[-1].start()
    for copy in copies:
        copy.wait()


def swap(value, step, count):
    return lax.ppermute(value, "row", [(i, i ^ step) for i in range(count)])


def on_device(site_cells, site_scale, panel):
    width = site_cells.shape[2]
    n_row = lax.axis_size("row")
    n_col = lax.axis_size("col")
    tiles = n_row // n_col
    share = width // n_col
    vmem = pl.BlockSpec(memory_space=pltpu.VMEM)
    packed = pl.pallas_call(
        pack,
        out_shape=pltpu.VMEM((4, width), jnp.float32),
        in_specs=[vmem, vmem],
        out_specs=vmem,
    )(site_cells, site_scale)
    if n_row == 8:
        arrived = [packed] + [swap(packed, k, n_row) for k in range(2, n_row, 2)]
        others = [swap(value, 1, n_row) for value in arrived]
        arrived = [value for both in zip(arrived, others) for value in both]
    else:
        arrived = [lax.all_gather(packed, "row", axis=0)]
    held = share if share % BLOCK == 0 else width
    lower, update = pl.pallas_call(
        functools.partial(kernel, n_col, share, len(arrived)),
        out_shape=(
            jax.ShapeDtypeStruct((width, held), jnp.float32),
            jax.ShapeDtypeStruct((width, tiles, width), jnp.bfloat16),
        ),
        in_specs=[pl.BlockSpec(memory_space=pltpu.SMEM)] + [vmem] * len(arrived),
        out_specs=(pl.BlockSpec(memory_space=pl.ANY),) * 2,
        scratch_shapes=[
            pltpu.VMEM((width, held), jnp.float32),
            pltpu.VMEM((width, tiles, width), jnp.bfloat16),
            pltpu.SemaphoreType.DMA((1 + width // BLOCK,)),
            pltpu.VMEM((width, width), jnp.float32),
            pltpu.VMEM((width, (1 + tiles) * width), jnp.float32),
            pltpu.VMEM((width, tiles * width), jnp.float32),
            pltpu.VMEM((2, width, 3 * width // 2), jnp.bfloat16),
            pltpu.VMEM((2, 3 * width // 2, (1 + tiles) * width), jnp.bfloat16),
            pltpu.VMEM((5, 2 * BLOCK, 6 * BLOCK), jnp.bfloat16),
            pltpu.VMEM((4, BLOCK, BLOCK), jnp.float32),
            pltpu.VMEM((2 + tiles, 8, width), jnp.float32),
            pltpu.VMEM((width, BLOCK), jnp.float32),
            pltpu.VMEM((2, width, 8), jnp.float32),
            pltpu.VMEM((n_row, 4, width), jnp.float32),
        ],
        compiler_params=pltpu.CompilerParams(vmem_limit_bytes=40 * 2**20),
    )(panel, *arrived)
    if held != share:
        lower = lax.dynamic_slice_in_dim(lower, lax.axis_index("col") * share, share, 1)
    return lower[None], update[None]


def solution(mesh):
    placed = (P(None, None, "row"), P(None, "row"), P())
    return jax.shard_map(
        on_device,
        mesh=mesh,
        in_specs=placed,
        out_specs=(P(None, "row", "col"), P(None, "row", None, "col")),
        check_vma=False,
    )
```
